256 devices in a mesh: ctx: 64 (over z, y, x_lo), head: 2 (over core), conv: 2 (over x_hi).
Axes of the slice: x: 4 (x_hi: 2, x_lo: 2; x = x_hi * 2 + x_lo), y: 4, z: 8, core: 2. Of those that a mesh axis runs over, the one named last changes fastest.
Arguments:
- queries: bfloat16 [4, 512, 8192], P('conv', 'ctx', 'head'), parts along dimension 0, may hold values from -100 to 100
- new_keys: bfloat16 [4, 512, 1024], P('conv', 'ctx', 'head'), parts along dimension 0, may hold values from -5.5 to 5.5
- incoming_values: bfloat16 [4, 512, 1024], P('conv', 'ctx', 'head'), parts along dimension 0, may hold values from -6 to 6
- slotted_cache_keys: bfloat16 [4, 256, 128, 1024], P('conv', 'ctx', None, 'head'), parts along dimension 0, may hold values from -6 to 6
- slotted_cache_values: bfloat16 [4, 256, 128, 1024], P('conv', 'ctx', None, 'head'), parts along dimension 0, may hold values from -6 to 6
- lengths: int32 [4], P('conv'), parts along dimension 0, may hold values from 8064 to 32256, as said below
- span_slots: int32 [4, 256], P('conv'), parts along dimension 0, may hold values from 0 to 255, as said below
Outputs:
- attended: bfloat16 [4, 512, 8192], P('conv', 'ctx', 'head'), parts along dimension 0
- cache_keys_out: bfloat16 [4, 256, 128, 1024], P('conv', 'ctx', None, 'head'), parts along dimension 0
- cache_values_out: bfloat16 [4, 256, 128, 1024], P('conv', 'ctx', None, 'head'), parts along dimension 0
The draws below stay inside these ranges and needn't reach their ends.
There are 2 independent parts, one for each index of `conv`. The reference program is written for one: setup_inputs(seed, part) draws one part's arguments, and reference() takes and returns one part's arrays. A program takes and returns all parts, laid end to end along the dimension named above; each array names one. Nothing has to cross between parts.
Inputs may be any that keep to these rules, and one draw needn't show every extreme that they name: `lengths`: in every part one conversation has exactly 32256 cached tokens. `span_slots`: each row is a permutation of the slots. Slot s lies on cycle member s // 4. Span j of a conversation lies on cycle member (j + r) mod (64) in its local slot j // 64, for a rotation r of that conversation.
All inputs are finite; a program needn't handle non-finite values.
Results may differ from the reference program's by a relative error of at most 0.013.
Values may be sent and summed in bfloat16 or wider, within the bound.
No kernel may reach another device: no remote copies, remote signals or barrier semaphores. Data moves between devices by JAX's collectives and lax.ppermute only.
A program may use at most 128 MiB of HBM per device.

```python
import math
import jax
import jax.numpy as jnp
from jax import lax

HEAD_SIZE = 128
QUERY_HEADS = 64
KEY_VALUE_HEADS = 8
PART_CONVERSATIONS = 2
TURN_TOKENS = 512
SPAN_TOKENS = 128
CPD = 4
CACHE_SLOTS = 256
CTX_MAX = 32256


def shared_turn(seed_key):
    random_streams = jax.random.split(seed_key, 2)
    base_queries = jnp.clip(jax.random.normal(random_streams[0], (PART_CONVERSATIONS, TURN_TOKENS, QUERY_HEADS, HEAD_SIZE), jnp.float32), -5.0, 5.0)
    starting_keys = jnp.clip(jax.random.normal(random_streams[1], (PART_CONVERSATIONS, TURN_TOKENS, KEY_VALUE_HEADS, HEAD_SIZE), jnp.float32), -5.0, 5.0)
    return (base_queries, starting_keys)


def draw_queries(seed_key, part_index):
    base_queries, starting_keys = shared_turn(seed_key)
    attention_output = base_queries
    return attention_output.reshape(PART_CONVERSATIONS, TURN_TOKENS, QUERY_HEADS * HEAD_SIZE).astype(jnp.bfloat16)


def draw_new_keys(seed_key, part_index):
    base_queries, starting_keys = shared_turn(seed_key)
    attention_output = starting_keys
    return attention_output.reshape(PART_CONVERSATIONS, TURN_TOKENS, KEY_VALUE_HEADS * HEAD_SIZE).astype(jnp.bfloat16)


def draw_lengths(seed_key, part_index):
    seed_key = jax.random.fold_in(seed_key, 5)
    random_streams = jax.random.split(seed_key, 2)
    drawn = jax.random.randint(random_streams[0], (PART_CONVERSATIONS,), CTX_MAX // 4, CTX_MAX + 1)
    longest = jax.random.randint(random_streams[1], (), 0, PART_CONVERSATIONS)
    return jnp.where(jnp.arange(PART_CONVERSATIONS) == longest, CTX_MAX, drawn).astype(jnp.int32)


def draw_span_slots(seed_key, part_index):
    seed_key = jax.random.fold_in(seed_key, 7)
    members = CACHE_SLOTS // CPD
    rotation = jax.random.randint(seed_key, (PART_CONVERSATIONS, 1), 0, members)
    span_index = jnp.arange(CACHE_SLOTS)[None, :]
    return ((span_index + rotation) % members * CPD + span_index // members).astype(jnp.int32)


def steps_of(key, dims, pieces, low, top_value):
    factor_of = 1.0
    for position, blocks in pieces:
        draws = jax.random.uniform(jax.random.fold_in(jax.random.fold_in(key, 6), position), (blocks,), jnp.float32, low / len(pieces), top_value / len(pieces))
        factor_of = factor_of * jnp.repeat(jnp.exp(draws), dims[position] // blocks).reshape((-1,) + (1,) * (len(dims) - 1 - position))
    return factor_of


def noise(key, extent, deviation, reach, shards=(), kind=jnp.bfloat16):
    values = deviation * jax.random.normal(key, extent, jnp.float32)
    if shards:
        values = values * steps_of(key, extent, shards, -0.22, 0.18)
    return jnp.clip(values, -reach, reach).astype(kind)


def setup_inputs(seed: int = 0, part: int = 0) -> dict:
    key_of = jax.random.split(jax.random.key(seed), 8)
    part_keys = jax.random.split(jax.random.fold_in(key_of[7], part), 8)
    queries = draw_queries(jax.random.fold_in(jax.random.fold_in(key_of[7], part), 71), part)
    new_keys = draw_new_keys(jax.random.fold_in(jax.random.fold_in(key_of[7], part), 71), part)
    incoming_values = noise(part_keys[2], (PART_CONVERSATIONS, TURN_TOKENS, KEY_VALUE_HEADS * HEAD_SIZE), 1.0, 6.0, ((1, 64), (2, 2)))
    slotted_cache_keys = noise(part_keys[3], (PART_CONVERSATIONS, CACHE_SLOTS, SPAN_TOKENS, KEY_VALUE_HEADS * HEAD_SIZE), 1.0, 6.0, ((1, 64), (3, 2)))
    slotted_cache_values = noise(part_keys[4], (PART_CONVERSATIONS, CACHE_SLOTS, SPAN_TOKENS, KEY_VALUE_HEADS * HEAD_SIZE), 1.0, 6.0, ((1, 64), (3, 2)))
    lengths = draw_lengths(jax.random.fold_in(jax.random.fold_in(key_of[7], part), 71), part)
    span_slots = draw_span_slots(jax.random.fold_in(jax.random.fold_in(key_of[7], part), 71), part)
    return dict(queries=queries, new_keys=new_keys, incoming_values=incoming_values, slotted_cache_keys=slotted_cache_keys, slotted_cache_values=slotted_cache_values, lengths=lengths, span_slots=span_slots)


NEG_LARGE = -1e+30

def block_attention(arguments):
    query_block, keys_head, values_head, limit_block = arguments
    scores = jnp.einsum('tgd,pd->tgp', query_block.astype(jnp.float32), keys_head.astype(jnp.float32)) * (1.0 / math.sqrt(HEAD_SIZE))
    places = jnp.arange(keys_head.shape[0], dtype=jnp.int32)
    allowed = places[None, None, :] <= limit_block[:, None, None]
    row_top = lax.optimization_barrier(jnp.max(jnp.where(allowed, scores, NEG_LARGE), axis=2))
    weights = jnp.where(allowed, jnp.exp(scores - row_top[:, :, None]), 0.0)
    totals = lax.optimization_barrier(jnp.sum(weights, axis=2))
    rounded = weights.astype(jnp.bfloat16)
    numerator = jnp.einsum('tgp,pd->tgd', rounded.astype(jnp.float32), values_head.astype(jnp.float32))
    return numerator / totals[:, :, None]

def one_conversation(arguments):
    rows_of_queries, key_rows, value_rows, slot_keys, slot_values, length, slots = arguments
    width = slot_keys.shape[-1]
    complete_rows = CACHE_SLOTS * SPAN_TOKENS
    start = length.astype(jnp.int32)
    anchor = jnp.zeros((), jnp.int32)
    ordered_keys = lax.dynamic_update_slice(slot_keys[slots].reshape(complete_rows, width), key_rows, (start, anchor))
    ordered_values = lax.dynamic_update_slice(slot_values[slots].reshape(complete_rows, width), value_rows, (start, anchor))
    keys_out = jnp.zeros_like(slot_keys).at[slots].set(ordered_keys.reshape(CACHE_SLOTS, SPAN_TOKENS, width))
    values_out = jnp.zeros_like(slot_values).at[slots].set(ordered_values.reshape(CACHE_SLOTS, SPAN_TOKENS, width))
    query_group_size = QUERY_HEADS // KEY_VALUE_HEADS
    tokens_block = min(64, TURN_TOKENS)
    limits = start + jnp.arange(TURN_TOKENS, dtype=jnp.int32)
    heads_of_queries = rows_of_queries.reshape(TURN_TOKENS // tokens_block, tokens_block, KEY_VALUE_HEADS, query_group_size, HEAD_SIZE).transpose(2, 0, 1, 3, 4)
    heads_of_keys = ordered_keys.reshape(complete_rows, KEY_VALUE_HEADS, HEAD_SIZE).transpose(1, 0, 2)
    heads_of_values = ordered_values.reshape(complete_rows, KEY_VALUE_HEADS, HEAD_SIZE).transpose(1, 0, 2)
    limit_blocks = limits.reshape(TURN_TOKENS // tokens_block, tokens_block)

    def one_head(head_args):
        query_head, keys_head, values_head = head_args
        return lax.map(lambda block_args: block_attention((block_args[0], keys_head, values_head, block_args[1])), (query_head, limit_blocks))
    attended = lax.map(one_head, (heads_of_queries, heads_of_keys, heads_of_values))
    attended = attended.transpose(1, 2, 0, 3, 4).reshape(TURN_TOKENS, QUERY_HEADS * HEAD_SIZE).astype(jnp.bfloat16)
    return (attended, keys_out, values_out)

def reference(queries, new_keys, incoming_values, slotted_cache_keys, slotted_cache_values, lengths, span_slots):
    results = lax.map(one_conversation, (queries, new_keys, incoming_values, slotted_cache_keys, slotted_cache_values, lengths, span_slots))
    return (results[0], results[1], results[2])
```

```python
import functools
import math

import jax
import jax.numpy as jnp
from jax import lax
from jax.experimental import pallas as pl
from jax.experimental.pallas import tpu as pltpu
from jax.sharding import Mesh, PartitionSpec as P

HEAD_SIZE = 128
NEG_LARGE = -1e30
SCALE = math.log2(math.e) / math.sqrt(HEAD_SIZE)
F32, BF16 = jnp.float32, jnp.bfloat16
MIB = 2**20
SUM_ROWS = 16


def dot(a, b):
    return jnp.dot(a, b, preferred_element_type=F32)


def pack_kernel(keys_ref, values_ref, out_ref):
    for head in range(out_ref.shape[0]):
        lanes = slice(head * HEAD_SIZE, (head + 1) * HEAD_SIZE)
        out_ref[head, 0, 0] = keys_ref[0, 0, :, lanes]
        out_ref[head, 1, 0] = values_ref[0, 0, :, lanes].T


def pack(cache_keys, cache_values):
    conv_count, slots, span, width = cache_keys.shape
    heads = width // HEAD_SIZE
    spec = pl.BlockSpec((1, 1, span, width), lambda c, s: (c, s, 0, 0))
    return pl.pallas_call(
        pack_kernel,
        grid=(conv_count, slots),
        in_specs=[spec, spec],
        out_specs=pl.BlockSpec((heads, 2, 1, span, HEAD_SIZE), lambda c, s: (c, 0, s, 0, 0)),
        out_shape=jax.ShapeDtypeStruct((conv_count * heads, 2, slots, span, HEAD_SIZE), BF16),
        name="pack",
    )(cache_keys, cache_values)


def attend_kernel(group, turn_part, scalars, q_ref, kv_ref, new_ref, o_ref, keys, sums):
    step = pl.program_id(0)
    sources, _, slots, span, _ = kv_ref.shape
    blocks = sources * slots
    cached = blocks * span
    length, me, good = scalars[blocks], scalars[blocks + 1], scalars[blocks + 2]

    @pl.when(step == 0)
    def _():
        filler = kv_ref[good, 0, 0, 0:16, :].astype(F32)[0:1]
        for s in range(sources):
            for j in range(slots):
                n = s * slots + j
                base = scalars[n]
                at = slice(n * span, (n + 1) * span)
                rows = lax.broadcasted_iota(jnp.int32, (span, HEAD_SIZE), 0) + base < length
                cols = lax.broadcasted_iota(jnp.int32, (HEAD_SIZE, span), 1) + base < length
                keys[at, :] = jnp.where(rows, kv_ref[s, 0, j].astype(F32), filler).astype(BF16)
                sums[0:HEAD_SIZE, at] = jnp.where(cols, kv_ref[s, 1, j].astype(F32), 0.0).astype(BF16)
                sums[HEAD_SIZE:, at] = jnp.where(cols[:SUM_ROWS], 1.0, 0.0).astype(BF16)
        keys[cached:, :] = new_ref[0:turn_part, :]
        sums[0:HEAD_SIZE, cached:] = new_ref[turn_part:, :].T
        sums[HEAD_SIZE:, cached:] = jnp.ones((SUM_ROWS, turn_part), BF16)

    chunks, _, width = q_ref.shape
    columns = chunks * width
    q = jnp.concatenate([q_ref[c] for c in range(chunks)], axis=1)
    top = jnp.full((1, columns), NEG_LARGE, F32)
    total = jnp.zeros((HEAD_SIZE + SUM_ROWS, columns), F32)
    tile = 512
    for j in range(0, cached + 1, tile):
        if j < cached:
            at = slice(j, j + tile)
            scores = dot(keys[at, :], q) * SCALE
        else:
            at = slice(cached, cached + turn_part)
            scores = dot(keys[at, :], q) * SCALE
            shape = scores.shape
            lane = lax.broadcasted_iota(jnp.int32, shape, 1)
            chunk = lane // width
            part = lax.rem(me + step * chunks + chunk, group)
            token = part * turn_part + (lane - chunk * width) // (width // turn_part)
            place = me * turn_part + lax.broadcasted_iota(jnp.int32, shape, 0)
            scores = jnp.where(place <= token, scores, NEG_LARGE)
        higher = jnp.maximum(top, jnp.max(scores, axis=0, keepdims=True))
        weights = jnp.exp2(scores - higher).astype(BF16)
        total = total * jnp.exp2(top - higher) + dot(sums[:, at], weights)
        top = higher
    denominator = total[HEAD_SIZE : HEAD_SIZE + 1]
    out = (total[:HEAD_SIZE] * (1.0 / denominator)).astype(BF16)
    level = top + jnp.log2(denominator)
    first = level.astype(BF16)
    rest = level - first.astype(F32)
    second = rest.astype(BF16)
    third = (rest - second.astype(F32)).astype(BF16)
    row = lax.broadcasted_iota(jnp.int32, (SUM_ROWS, columns), 0)
    coded = jnp.where(
        row == 0, first.astype(F32), jnp.where(row == 1, second.astype(F32), third.astype(F32))
    ).astype(BF16)
    for c in range(chunks):
        o_ref[c, 0:HEAD_SIZE] = out[:, c * width : (c + 1) * width]
        o_ref[c, HEAD_SIZE:] = coded[:, c * width : (c + 1) * width]


def attend(scalars, chunks, kv, new, group, turn_part):
    count, _, width = chunks.shape
    width = width - 128
    per_step = 2
    cached = kv.shape[0] * kv.shape[2] * kv.shape[3]
    whole = lambda i, s: (0, 0, 0, 0, 0)
    return pl.pallas_call(
        functools.partial(attend_kernel, group, turn_part),
        grid_spec=pltpu.PrefetchScalarGridSpec(
            num_scalar_prefetch=1,
            grid=(count // per_step,),
            in_specs=[
                pl.BlockSpec((per_step, HEAD_SIZE, width), lambda i, s: (i, 0, 0)),
                pl.BlockSpec(kv.shape, whole),
                pl.BlockSpec(new.shape, lambda i, s: (0, 0)),
            ],
            out_specs=pl.BlockSpec(
                (per_step, HEAD_SIZE + SUM_ROWS, width), lambda i, s: (i, 0, 0)
            ),
            scratch_shapes=[
                pltpu.VMEM((cached + turn_part, HEAD_SIZE), BF16),
                pltpu.VMEM((HEAD_SIZE + SUM_ROWS, cached + turn_part), BF16),
            ],
        ),
        out_shape=jax.ShapeDtypeStruct((count, HEAD_SIZE + SUM_ROWS, width), BF16),
        compiler_params=pltpu.CompilerParams(vmem_limit_bytes=40 * MIB),
        cost_estimate=pl.CostEstimate(
            flops=4 * HEAD_SIZE * count * width * cached,
            bytes_accessed=5 * MIB,
            transcendentals=count * width * cached,
        ),
        name="attend",
    )(scalars, chunks, kv, new)


def merge_kernel(*refs):
    parts, out_ref = refs[:-1], refs[-1]
    levels = []
    for part in parts:
        coded = part[HEAD_SIZE:].astype(F32)
        levels.append(coded[0:1] + coded[1:2] + coded[2:3])
    top = functools.reduce(jnp.maximum, levels)
    shares = [jnp.exp2(level - top) for level in levels]
    over = 1.0 / functools.reduce(jnp.add, shares)
    out = functools.reduce(
        jnp.add,
        [part[:HEAD_SIZE].astype(F32) * (share * over) for part, share in zip(parts, shares)],
    )
    out_ref[...] = out.T.astype(BF16)


def merge(parts):
    width = parts[0].shape[1]
    return pl.pallas_call(
        merge_kernel,
        out_shape=jax.ShapeDtypeStruct((width, HEAD_SIZE), BF16),
        name="merge",
    )(*parts)


def shift(x, axis, size, by):
    return lax.ppermute(x, axis, [(i, (i + by) % size) for i in range(size)])


def gather_ring(x, axis, size):
    held = {0: x}
    for step in range(1, size // 2):
        held[size - step] = shift(held[(size - step + 1) % size], axis, size, 1)
        held[step] = shift(held[step - 1], axis, size, -1)
    half = x.shape[0] // 2
    below = shift(held[size // 2 + 1][:half], axis, size, 1)
    above = shift(held[size // 2 - 1][half:], axis, size, -1)
    held[size // 2] = jnp.concatenate([below, above], axis=0)
    return jnp.stack([held[i] for i in range(size)])


def on_device(rows, columns, queries, new_keys, new_values, cache_keys, cache_values, lengths, span_slots):
    convs, tokens, query_width = queries.shape
    heads = new_keys.shape[2] // HEAD_SIZE
    per_head = query_width // (heads * HEAD_SIZE)
    slots, span = cache_keys.shape[1:3]
    pairs = convs * heads
    cycle = rows * columns
    turn_part = columns * tokens
    turn = rows * turn_part
    z, b = lax.axis_index("z"), lax.axis_index("b")

    kv = lax.all_to_all(pack(cache_keys, cache_values), "b", 0, 0, tiled=True)

    def by_pair(x, inner):
        return (
            x.reshape(convs, tokens, heads, inner, HEAD_SIZE)
            .transpose(0, 2, 1, 3, 4)
            .reshape(pairs, tokens * inner, HEAD_SIZE)
        )

    turn_rows = jnp.concatenate(
        [by_pair(queries, per_head), by_pair(new_keys, 1), by_pair(new_values, 1)], axis=1
    )
    turn_rows = lax.all_to_all(turn_rows, "b", 0, 0, tiled=True)
    q_rows = tokens * per_head
    own_q = turn_rows[:, :q_rows].reshape(columns * q_rows, HEAD_SIZE)
    own_new = turn_rows[:, q_rows:].reshape(columns, 2, tokens, HEAD_SIZE)
    own_new = own_new.transpose(1, 0, 2, 3).reshape(2 * turn_part, HEAD_SIZE)
    chunks = gather_ring(jnp.concatenate([own_q.T, own_new], axis=1), "z", rows)

    rotation = span_slots[:, 0] // slots
    conv = b // heads
    length = lengths[conv]
    member = z * columns + jnp.arange(columns, dtype=jnp.int32)
    first_span = jnp.mod(member - rotation[conv], cycle)
    bases = (first_span[:, None] + cycle * jnp.arange(slots, dtype=jnp.int32)) * span
    good = jnp.where(bases[0, 0] < length, 0, 1)
    scalars = jnp.concatenate([bases.reshape(-1), jnp.stack([length, z, good])]).astype(jnp.int32)

    parts = attend(scalars, chunks, kv, own_new, rows, turn_part)

    def turn_slot(members, conv_length, conv_rotation):
        spans = jnp.mod(members - conv_rotation, cycle)
        at = (conv_length // span - spans + cycle - 1) // cycle
        at = jnp.clip(at, 0, slots - 1)
        return at, (spans + at * cycle) * span - conv_length

    all_new = jnp.roll(chunks[:, :, q_rows * columns :], z, axis=0)
    all_new = all_new.reshape(rows, 2, turn_part, HEAD_SIZE)
    all_new = all_new.transpose(0, 2, 1, 3).reshape(turn, 2 * HEAD_SIZE)
    padded = jnp.pad(all_new, ((span, span), (0, 0)))
    _, starts = turn_slot(member, length, rotation[conv])
    starts = jnp.clip(starts + span, 0, turn + span)
    windows = jnp.stack(
        [lax.dynamic_slice(padded, (starts[i], 0), (span, 2 * HEAD_SIZE)) for i in range(columns)]
    )
    windows = lax.all_to_all(windows, "b", 0, 0, tiled=True)
    windows = windows.reshape(convs, heads, span, 2, HEAD_SIZE).transpose(3, 0, 2, 1, 4)
    windows = windows.reshape(2, convs, 1, span, heads * HEAD_SIZE)
    slot, start = turn_slot(z * columns + b, lengths, rotation)
    token = start[:, None] + jnp.arange(span, dtype=jnp.int32)
    fresh = (token >= 0) & (token < turn)
    here = jnp.arange(slots, dtype=jnp.int32)[None, :] == slot[:, None]
    fresh = (fresh[:, None, :] & here[:, :, None])[..., None]
    keys_out = jnp.where(fresh, windows[0], cache_keys)
    values_out = jnp.where(fresh, windows[1], cache_values)

    received = [parts[0]] + [shift(parts[i], "z", rows, i) for i in range(1, rows)]
    done = merge(received).reshape(columns, q_rows, HEAD_SIZE)
    done = lax.all_to_all(done, "b", 0, 0, tiled=True)
    attended = (
        done.reshape(convs, heads, tokens, per_head, HEAD_SIZE)
        .transpose(0, 2, 1, 3, 4)
        .reshape(convs, tokens, query_width)
    )
    return attended, keys_out, values_out


def solution(mesh):
    members, heads, convs = mesh.devices.shape
    columns = 8
    rows = members // columns
    grid = Mesh(mesh.devices.reshape(rows, columns, heads, convs), ("z", "b", "head", "conv"))
    ctx = ("z", "b")
    turn = P("conv", ctx, "head")
    cache = P("conv", ctx, None, "head")
    return jax.shard_map(
        functools.partial(on_device, rows, columns),
        mesh=grid,
        in_specs=(turn, turn, turn, cache, cache, P("conv"), P("conv", None)),
        out_specs=(turn, cache, cache),
        check_vma=False,
    )
```

```python
import functools
import math

import jax
import jax.numpy as jnp
from jax import lax
from jax.experimental import pallas as pl
from jax.experimental.pallas import tpu as pltpu
from jax.sharding import Mesh, PartitionSpec as P

HEAD = 128
LOWEST = -1e30
SCALE = math.log2(math.e) / math.sqrt(HEAD)
F32, BF16, I32 = jnp.float32, jnp.bfloat16, jnp.int32
MIB = 2**20
EXTRA = 16
TILE = 512
COLUMNS = 8
SMEM = pl.BlockSpec(memory_space=pltpu.SMEM)
VMEM = pl.BlockSpec(memory_space=pltpu.VMEM)
ANY = pl.BlockSpec(memory_space=pl.ANY)

def dot(a, b):
    return jnp.dot(a, b, preferred_element_type=F32)


def shift(a, by, size=8):
    return lax.ppermute(a, "z", [(i, (i + by) % size) for i in range(size)])


def pack_turn_kernel(q_ref, k_ref, v_ref, out_ref):
    convs, tokens, width = q_ref.shape
    heads = k_ref.shape[2] // HEAD
    group = width // (heads * HEAD)
    for c in range(convs):
        for h in range(heads):
            pieces = []
            for g in range(group):
                at = (h * group + g) * HEAD
                pieces.append(q_ref[c, :, at : at + HEAD])
            pieces.append(k_ref[c, :, h * HEAD : (h + 1) * HEAD])
            pieces.append(v_ref[c, :, h * HEAD : (h + 1) * HEAD])
            out_ref[c * heads + h] = jnp.concatenate(pieces, axis=0)


def pack_turn(queries, new_keys, new_values):
    convs, tokens, width = queries.shape
    heads = new_keys.shape[2] // HEAD
    rows = tokens * (width // (heads * HEAD) + 2)
    return pl.pallas_call(
        pack_turn_kernel,
        in_specs=[VMEM] * 3,
        out_specs=VMEM,
        out_shape=jax.ShapeDtypeStruct((convs * heads, rows, HEAD), BF16),
        compiler_params=pltpu.CompilerParams(vmem_limit_bytes=6 * MIB),
        name="pack_turn",
    )(queries, new_keys, new_values)


def ring_message_kernel(rows_ref, out_ref, new_ref):
    columns, count, _ = rows_ref.shape
    tokens = 8
    q_rows = count - 2 * tokens
    q = jnp.concatenate([rows_ref[s, 0:q_rows] for s in range(columns)], axis=0)
    keys = [rows_ref[s, q_rows : q_rows + tokens] for s in range(columns)]
    values = [rows_ref[s, q_rows + tokens :] for s in range(columns)]
    new = jnp.concatenate(keys + values, axis=0)
    out_ref[:, 0 : columns * q_rows] = q.T
    out_ref[:, columns * q_rows :] = new
    new_ref[...] = new


def ring_message(rows):
    columns, count, _ = rows.shape
    width = columns * (count - 16)
    return pl.pallas_call(
        ring_message_kernel,
        in_specs=[VMEM],
        out_specs=[VMEM, VMEM],
        out_shape=[
            jax.ShapeDtypeStruct((HEAD, width + HEAD), BF16),
            jax.ShapeDtypeStruct((HEAD, HEAD), BF16),
        ],
        compiler_params=pltpu.CompilerParams(vmem_limit_bytes=6 * MIB),
        name="ring_message",
    )(rows)


def pack_cache_kernel(keys_ref, values_ref, *rest):
    outs, sems = rest[:-1], rest[-1]
    convs, slots, _, width = keys_ref.shape
    heads = width // HEAD
    per_out = slots // len(outs)
    copies = []
    for c in range(convs):
        for h in range(heads):
            for i, ref in enumerate((keys_ref, values_ref)):
                for n, out in enumerate(outs):
                    held = pl.ds(n * per_out, per_out)
                    copy = pltpu.make_async_copy(
                        ref.at[c, held, :, pl.ds(h * HEAD, HEAD)],
                        out.at[c * heads + h, i],
                        sems.at[len(copies)],
                    )
                    copy.start()
                    copies.append(copy)
    for copy in copies:
        copy.wait()


def pack_cache(cache_keys, cache_values, count):
    convs, slots, span, width = cache_keys.shape
    pairs = convs * width // HEAD
    return pl.pallas_call(
        pack_cache_kernel,
        in_specs=[ANY, ANY],
        out_specs=[VMEM] * count,
        out_shape=[jax.ShapeDtypeStruct((pairs, 2, slots // count, span, HEAD), BF16)] * count,
        scratch_shapes=[pltpu.SemaphoreType.DMA((2 * pairs * count,))],
        compiler_params=pltpu.CompilerParams(vmem_limit_bytes=8 * MIB),
        name="pack_cache",
    )(cache_keys, cache_values)


def prepare_kernel(first_slot, cycle, place, lengths, slots_ref, kv, *refs):
    rest, keys, sums = refs[:-2], refs[-2], refs[-1]
    sources, _, slots, span, _ = kv.shape
    all_slots = slots_ref.shape[1] // cycle
    z, b = place[0], place[1]
    conv = b // (COLUMNS // 2)
    length = lengths[conv]
    rotation = slots_ref[conv, 0] // all_slots
    cached = sources * slots * span

    def base(source, slot):
        member = z * COLUMNS + source
        return (slot * cycle + lax.rem(member - rotation + cycle, cycle)) * span

    if rest:
        new_ref, known = rest
        filler = known[0:16, :].astype(F32)[0:1]
    else:
        first = kv[0, 0, 0, 0:16, :].astype(F32)[0:1]
        second = kv[1, 0, 0, 0:16, :].astype(F32)[0:1]
        filler = jnp.where(base(0, 0) < length, first, second)
    for source in range(sources):
        for slot in range(slots):
            left = length - base(source, first_slot + slot)
            start = (source * slots + slot) * span
            at = slice(start, start + span)
            rows = lax.broadcasted_iota(I32, (span, HEAD), 0) < left
            cols = lax.broadcasted_iota(I32, (HEAD, span), 1) < left
            keys[at, :] = jnp.where(rows, kv[source, 0, slot].astype(F32), filler).astype(BF16)
            turned = kv[source, 1, slot].T.astype(F32)
            sums[0:HEAD, at] = jnp.where(cols, turned, 0.0).astype(BF16)
            sums[HEAD:, at] = jnp.where(cols[:EXTRA], 1.0, 0.0).astype(BF16)
    if rest:
        turn_part = new_ref.shape[0] // 2
        keys[cached:, :] = new_ref[0:turn_part, :]
        sums[0:HEAD, cached:] = new_ref[turn_part:, :].T
        sums[HEAD:, cached:] = jnp.ones((EXTRA, turn_part), BF16)


def prepare(place, lengths, span_slots, first_slot, kv, cycle, new=None, known=None):
    positions = kv.shape[0] * kv.shape[2] * kv.shape[3]
    rest = []
    if new is not None:
        positions += new.shape[0] // 2
        rest = [new, known]
    return pl.pallas_call(
        functools.partial(prepare_kernel, first_slot, cycle),
        in_specs=[SMEM] * 3 + [VMEM] * (1 + len(rest)),
        out_specs=[VMEM] * 2,
        out_shape=[
            jax.ShapeDtypeStruct((positions, HEAD), BF16),
            jax.ShapeDtypeStruct((HEAD + EXTRA, positions), BF16),
        ],
        compiler_params=pltpu.CompilerParams(vmem_limit_bytes=12 * MIB),
        name="prepare",
    )(place, lengths, span_slots, kv, *rest)


def level_of(part):
    coded = part[HEAD:].astype(F32)
    return coded[0:1] + coded[1:2] + coded[2:3]


def combine(parts):
    levels = [level_of(part) for part in parts]
    top = functools.reduce(jnp.maximum, levels)
    shares = [jnp.exp2(level - top) for level in levels]
    total = functools.reduce(jnp.add, shares)
    sums = functools.reduce(
        jnp.add, [part[:HEAD].astype(F32) * share for part, share in zip(parts, shares)]
    )
    return sums, total, top


def attend_kernel(parts, distances, inits, with_new, *refs):
    count = len(distances)
    place, refs = refs[0], refs[1:]
    q_refs, refs = refs[:count], refs[count:]
    init_refs, refs = refs[: sum(inits)], refs[sum(inits) :]
    keys, sums, outs = refs[0], refs[1], refs[2:]
    width = outs[0].shape[1]
    columns = count * width
    turn_part = width // 8
    cached = keys.shape[0] - with_new * turn_part
    z = place[0]

    q = jnp.concatenate([ref[:, 0:width] for ref in q_refs], axis=1).astype(F32) * SCALE
    high = q.astype(BF16)
    low = (q - high.astype(F32)).astype(BF16)
    q = jnp.concatenate([high, low], axis=0)
    tops, totals, at_init = [], [], 0
    for given in inits:
        if given:
            held, weight, level = combine(init_refs[at_init : at_init + given])
            at_init += given
            tops.append(level)
            totals.append(
                jnp.concatenate([held, jnp.broadcast_to(weight, (EXTRA, width))], axis=0)
            )
        else:
            tops.append(jnp.full((1, width), LOWEST, F32))
            totals.append(jnp.zeros((HEAD + EXTRA, width), F32))
    top = jnp.concatenate(tops, axis=1)
    total = jnp.concatenate(totals, axis=1)
    tiles = [slice(j, j + TILE) for j in range(0, cached, TILE)]
    if with_new:
        tiles.append(slice(cached, cached + turn_part))

    def scores_of(at):
        twice = jnp.concatenate([keys[at, :]] * 2, axis=1)
        scores = dot(twice, q)
        if at.start < cached:
            return scores
        row = lax.broadcasted_iota(I32, (turn_part, width), 0)
        lane = lax.broadcasted_iota(I32, (turn_part, width), 1)
        token = (lane // 64) * 8 + lax.rem(lane, 8)
        ahead = jnp.concatenate(
            [row - token + (z - lax.rem(z + d, parts)) * turn_part for d in distances], axis=1
        )
        return jnp.where(ahead <= 0, scores, LOWEST)

    scores = scores_of(tiles[0])
    for n, at in enumerate(tiles):
        following = scores_of(tiles[n + 1]) if n + 1 < len(tiles) else None
        higher = jnp.maximum(top, jnp.max(scores, axis=0, keepdims=True))
        weights = jnp.exp2(scores - higher).astype(BF16)
        total = total * jnp.exp2(top - higher) + dot(sums[:, at], weights)
        top, scores = higher, following
    denominator = total[HEAD : HEAD + 1]
    out = (total[:HEAD] * (1.0 / denominator)).astype(BF16)
    level = top + jnp.log2(denominator)
    first = level.astype(BF16).astype(F32)
    second = (level - first).astype(BF16).astype(F32)
    third = level - first - second
    row = lax.broadcasted_iota(I32, (EXTRA, columns), 0)
    coded = jnp.where(row == 0, first, jnp.where(row == 1, second, third)).astype(BF16)
    for c in range(count):
        at = slice(c * width, (c + 1) * width)
        outs[c][0:HEAD] = out[:, at]
        outs[c][HEAD:] = coded[:, at]


def attend(place, kv, chunks, distances, inits, parts, with_new):
    keys, sums = kv
    count = len(distances)
    width = chunks[0].shape[1] - HEAD
    given = [part for init in inits for part in init]
    return pl.pallas_call(
        functools.partial(attend_kernel, parts, distances, [len(i) for i in inits], with_new),
        in_specs=[SMEM] + [VMEM] * (count + len(given) + 2),
        out_specs=[VMEM] * count,
        out_shape=[jax.ShapeDtypeStruct((HEAD + EXTRA, width), BF16)] * count,
        compiler_params=pltpu.CompilerParams(vmem_limit_bytes=16 * MIB),
        cost_estimate=pl.CostEstimate(
            flops=8 * HEAD * count * width * keys.shape[0],
            bytes_accessed=3 * MIB,
            transcendentals=count * width * keys.shape[0],
        ),
        name="attend",
    )(place, *chunks, *given, keys, sums)


def merge_kernel(*refs):
    parts, out_ref = refs[:-1], refs[-1]
    sums, total, _ = combine(parts)
    turned = (sums * (1.0 / total)).astype(BF16).T
    columns, rows, _ = out_ref.shape
    for s in range(columns):
        out_ref[s] = turned[s * rows : (s + 1) * rows]


def merge(parts):
    width = parts[0].shape[1]
    return pl.pallas_call(
        merge_kernel,
        in_specs=[VMEM] * len(parts),
        out_specs=VMEM,
        out_shape=jax.ShapeDtypeStruct((COLUMNS, width // COLUMNS, HEAD), BF16),
        compiler_params=pltpu.CompilerParams(vmem_limit_bytes=8 * MIB),
        name="merge",
    )(*parts)


def unpack_kernel(rows_ref, out_ref):
    convs, tokens, width = out_ref.shape
    pairs, rows, _ = rows_ref.shape
    heads, group = pairs // convs, rows // tokens
    for c in range(convs):
        for h in range(heads):
            for g in range(group):
                at = (h * group + g) * HEAD
                piece = rows_ref[c * heads + h, g * tokens : (g + 1) * tokens]
                out_ref[c, :, at : at + HEAD] = piece


def unpack(rows, shape):
    return pl.pallas_call(
        unpack_kernel,
        out_shape=jax.ShapeDtypeStruct(shape, BF16),
        compiler_params=pltpu.CompilerParams(vmem_limit_bytes=6 * MIB),
        name="unpack",
    )(rows)


def turn_slot(length, rotation, member, slots, cycle, span):
    j = lax.rem(member - rotation + cycle, cycle)
    slot = jnp.clip((length // span - j + cycle - 1) // cycle, 0, slots - 1)
    return slot, (j + slot * cycle) * span - length


def windows_kernel(slots, span, cycle, place, lengths, slots_ref, *refs):
    chunks, out_ref, rows = refs[:-2], refs[-2], refs[-1]
    parts = len(chunks)
    width = chunks[0].shape[1] - HEAD
    turn_part = HEAD // 2
    turn = parts * turn_part
    z, b = place[0], place[1]
    conv = b // (COLUMNS // 2)
    rotation = slots_ref[conv, 0] // slots
    edge = jnp.zeros((span, 2 * HEAD), F32)
    rows[0:span] = edge
    rows[span + turn : turn + 2 * span] = edge
    rows[turn + 2 * span :] = edge[0:8]
    for d, chunk in enumerate(chunks):
        start = pl.multiple_of(span + lax.rem(z + d, parts) * turn_part, turn_part)
        rows[pl.ds(start, turn_part), 0:HEAD] = chunk[0:turn_part, width:].astype(F32)
        rows[pl.ds(start, turn_part), HEAD:] = chunk[turn_part:, width:].astype(F32)
    for to in range(COLUMNS):
        _, token = turn_slot(lengths[conv], rotation, z * COLUMNS + to, slots, cycle, span)
        start = jnp.clip(token + span, 0, turn + span)
        whole = pl.multiple_of(start // 8 * 8, 8)
        window = rows[pl.ds(whole, span + 8), :]
        window = pltpu.roll(window, lax.rem(span + 8 + whole - start, span + 8), 0)
        window = window[0:span].astype(BF16)
        out_ref[to, 0:span] = window[:, 0:HEAD]
        out_ref[to, span:] = window[:, HEAD:]


def windows(place, lengths, span_slots, chunks, slots, span, cycle):
    turn = len(chunks) * HEAD // 2
    return pl.pallas_call(
        functools.partial(windows_kernel, slots, span, cycle),
        in_specs=[SMEM] * 3 + [VMEM] * len(chunks),
        out_specs=VMEM,
        out_shape=jax.ShapeDtypeStruct((COLUMNS, 2 * span, HEAD), BF16),
        scratch_shapes=[pltpu.VMEM((turn + 2 * span + 8, 2 * HEAD), F32)],
        compiler_params=pltpu.CompilerParams(vmem_limit_bytes=8 * MIB),
        name="windows",
    )(place, lengths, span_slots, *chunks)


def write_kernel(turn, cycle, place, lengths, slots_ref, new_ref, k_ref, v_ref, ko_ref, vo_ref):
    conv = pl.program_id(0)
    _, slots, span, width = k_ref.shape
    heads = width // HEAD
    member = place[0] * COLUMNS + place[1]
    rotation = slots_ref[conv, 0] // slots
    slot, token = turn_slot(lengths[conv], rotation, member, slots, cycle, span)
    ko_ref[...] = k_ref[...]
    vo_ref[...] = v_ref[...]

    @pl.when((token > -span) & (token < turn))
    def _():
        row = lax.broadcasted_iota(I32, (span, HEAD), 0) + token
        inside = (row >= 0) & (row < turn)
        for h in range(heads):
            lanes = slice(h * HEAD, (h + 1) * HEAD)
            for i, (old, out) in enumerate(((k_ref, ko_ref), (v_ref, vo_ref))):
                new = new_ref[h, i * span : (i + 1) * span].astype(F32)
                kept = old[0, slot, :, lanes].astype(F32)
                out[0, slot, :, lanes] = jnp.where(inside, new, kept).astype(BF16)


def write(place, lengths, span_slots, new, cache_keys, cache_values, turn, cycle):
    convs, slots, span, width = cache_keys.shape
    spec = pl.BlockSpec((1, slots, span, width), lambda c: (c, 0, 0, 0))
    new_block = (new.shape[0] // convs,) + new.shape[1:]
    shape = jax.ShapeDtypeStruct(cache_keys.shape, BF16)
    return pl.pallas_call(
        functools.partial(write_kernel, turn, cycle),
        grid=(convs,),
        in_specs=[SMEM] * 3 + [pl.BlockSpec(new_block, lambda c: (c, 0, 0)), spec, spec],
        out_specs=[spec, spec],
        out_shape=[shape, shape],
        compiler_params=pltpu.CompilerParams(vmem_limit_bytes=12 * MIB),
        cost_estimate=pl.CostEstimate(flops=0, bytes_accessed=5 * MIB, transcendentals=0),
        name="write",
    )(place, lengths, span_slots, new, cache_keys, cache_values)


def on_device(parts, queries, new_keys, new_values, cache_keys, cache_values, lengths, span_slots):
    _, slots, span, _ = cache_keys.shape
    cycle = parts * COLUMNS
    place = jnp.stack([lax.axis_index("z"), lax.axis_index("b")]).astype(I32)
    tie = lax.optimization_barrier

    turn_rows = pack_turn(queries, new_keys, new_values)
    turn_rows, cache_k, cache_v = tie((turn_rows, cache_keys, cache_values))
    turn_rows = lax.all_to_all(turn_rows, "b", 0, 0, tiled=True)
    first, second = pack_cache(cache_k, cache_v, 2)
    turn_rows, first, second = tie((turn_rows, first, second))
    first = lax.all_to_all(first, "b", 0, 0, tiled=True)

    message, new = ring_message(turn_rows)
    chunks = [None] * parts
    chunks[0] = message
    half = message.shape[0] // 2

    def run(kv, distances, inits=None, after=()):
        held = [chunks[d] for d in distances]
        if after:
            held, _ = tie((held, after))
        inits = inits or [()] * len(distances)
        return attend(place, kv, held, distances, inits, parts, kv is far)

    far = None
    chunks[7], chunks[1] = shift(message, 1), shift(message, -1)
    second, first, chunks[7], chunks[1] = tie((second, first, chunks[7], chunks[1]))
    second = lax.all_to_all(second, "b", 0, 0, tiled=True)
    chunks[6], chunks[2] = shift(chunks[7], 1), shift(chunks[1], -1)
    near = prepare(place, lengths, span_slots, 0, first, cycle)
    own, a1, a7 = run(near, (0, 1, 7))
    chunks[6], chunks[2], own = tie((chunks[6], chunks[2], own))
    chunks[5], chunks[3] = shift(chunks[6], 1), shift(chunks[2], -1)
    a2, a6 = run(near, (2, 6))
    chunks[5], chunks[3], a2 = tie((chunks[5], chunks[3], a2))
    below, above = shift(chunks[5][:half], 1), shift(chunks[3][half:], -1)
    a3, a5 = run(near, (3, 5))
    below, above, a3, second = tie((below, above, a3, second))
    far = prepare(place, lengths, span_slots, slots // 2, second, cycle, new, near[0])
    chunks[4] = jnp.concatenate([below, above], axis=0)
    (a4,) = run(near, (4,))
    rows = windows(place, lengths, span_slots, chunks, slots, span, cycle)
    a4, rows = tie((a4, rows))

    up4, up3 = run(far, (4, 3), ((a4,), (a3,)))
    down3, own = run(far, (5, 0), ((a5,), (own,)), after=(up4,))
    up4, up3 = shift(up4, 2), shift(up3, 2)
    up2, down2 = run(far, (2, 6), ((a2, up4), (a6,)), after=(down3,))
    rows, _ = tie((rows, up2))
    rows = lax.all_to_all(rows, "b", 0, 0, tiled=True)
    down3 = shift(down3, -2)
    up1, down1 = run(far, (1, 7), ((a1, up3), (a7, down3)), after=(up2,))
    up2, down2 = shift(up2, 2), shift(down2, -2)
    up1, down1 = shift(up1, 1), shift(down1, -1)
    own, rows = tie((own, rows))
    done = merge([own, up2, down2, up1, down1])
    done = lax.all_to_all(done, "b", 0, 0, tiled=True)
    attended = unpack(done, queries.shape)
    keys_out, values_out = write(
        place, lengths, span_slots, rows, cache_keys, cache_values, parts * HEAD // 2, cycle
    )
    return attended, keys_out, values_out


def solution(mesh):
    members, heads, convs = mesh.devices.shape
    parts = members // COLUMNS
    grid = Mesh(mesh.devices.reshape(parts, COLUMNS, heads, convs), ("z", "b", "head", "conv"))
    ctx = ("z", "b")
    turn = P("conv", ctx, "head")
    cache = P("conv", ctx, None, "head")
    return jax.shard_map(
        functools.partial(on_device, parts),
        mesh=grid,
        in_specs=(turn, turn, turn, cache, cache, P("conv"), P("conv", None)),
        out_specs=(turn, cache, cache),
        check_vma=False,
    )
```

```python
import functools
import math

import jax
import jax.numpy as jnp
from jax import lax
from jax.experimental import pallas as pl
from jax.experimental.pallas import tpu as pltpu
from jax.sharding import Mesh, PartitionSpec as P

HEAD = 128
LOWEST = -1e30
SCALE = math.log2(math.e) / math.sqrt(HEAD)
F32, BF16, I32 = jnp.float32, jnp.bfloat16, jnp.int32
MIB = 2**20
EXTRA = 16
TILE = 512
COLUMNS = 8
SMEM = pl.BlockSpec(memory_space=pltpu.SMEM)
VMEM = pl.BlockSpec(memory_space=pltpu.VMEM)
ANY = pl.BlockSpec(memory_space=pl.ANY)
HBM = pl.BlockSpec(memory_space=pltpu.HBM)

def dot(a, b):
    return jnp.dot(a, b, preferred_element_type=F32)


def shift(a, by, size=8):
    return lax.ppermute(a, "z", [(i, (i + by) % size) for i in range(size)])


def pack_turn_kernel(*refs):
    sources, out_ref, held, sems = refs[:3], refs[3], refs[4:7], refs[7]
    copies = [
        pltpu.make_async_copy(source, target, sems.at[i])
        for i, (source, target) in enumerate(zip(sources, held))
    ]
    for copy in copies:
        copy.start()
    for copy in copies:
        copy.wait()
    q_ref, k_ref, v_ref = held
    convs, tokens, width = q_ref.shape
    heads = k_ref.shape[2] // HEAD
    group = width // (heads * HEAD)
    for c in range(convs):
        for h in range(heads):
            pieces = []
            for g in range(group):
                at = (h * group + g) * HEAD
                pieces.append(q_ref[c, :, at : at + HEAD])
            pieces.append(k_ref[c, :, h * HEAD : (h + 1) * HEAD])
            pieces.append(v_ref[c, :, h * HEAD : (h + 1) * HEAD])
            out_ref[c * heads + h] = jnp.concatenate(pieces, axis=0)


def pack_turn(queries, new_keys, new_values):
    convs, tokens, width = queries.shape
    heads = new_keys.shape[2] // HEAD
    rows = tokens * (width // (heads * HEAD) + 2)
    return pl.pallas_call(
        pack_turn_kernel,
        in_specs=[HBM] * 3,
        out_specs=VMEM,
        out_shape=jax.ShapeDtypeStruct((convs * heads, rows, HEAD), BF16),
        scratch_shapes=[pltpu.VMEM(x.shape, BF16) for x in (queries, new_keys, new_values)]
        + [pltpu.SemaphoreType.DMA((3,))],
        compiler_params=pltpu.CompilerParams(vmem_limit_bytes=60 * MIB),
        name="pack_turn",
    )(queries, new_keys, new_values)


def ring_message_kernel(rows_ref, out_ref, new_ref):
    columns, count, _ = rows_ref.shape
    tokens = 8
    q_rows = count - 2 * tokens
    q = jnp.concatenate([rows_ref[s, 0:q_rows] for s in range(columns)], axis=0)
    keys = [rows_ref[s, q_rows : q_rows + tokens] for s in range(columns)]
    values = [rows_ref[s, q_rows + tokens :] for s in range(columns)]
    new = jnp.concatenate(keys + values, axis=0)
    out_ref[:, 0 : columns * q_rows] = q.T
    out_ref[:, columns * q_rows :] = new
    new_ref[...] = new


def ring_message(rows):
    columns, count, _ = rows.shape
    width = columns * (count - 16)
    return pl.pallas_call(
        ring_message_kernel,
        in_specs=[VMEM],
        out_specs=[VMEM, VMEM],
        out_shape=[
            jax.ShapeDtypeStruct((HEAD, width + HEAD), BF16),
            jax.ShapeDtypeStruct((HEAD, HEAD), BF16),
        ],
        compiler_params=pltpu.CompilerParams(vmem_limit_bytes=6 * MIB),
        name="ring_message",
    )(rows)


def pack_cache_kernel(keys_ref, values_ref, *rest):
    outs, sems = rest[:-1], rest[-1]
    convs, slots, _, width = keys_ref.shape
    heads = width // HEAD
    per_out = slots // len(outs)
    copies = []
    for c in range(convs):
        for h in range(heads):
            for i, ref in enumerate((keys_ref, values_ref)):
                for n, out in enumerate(outs):
                    held = pl.ds(n * per_out, per_out)
                    copy = pltpu.make_async_copy(
                        ref.at[c, held, :, pl.ds(h * HEAD, HEAD)],
                        out.at[c * heads + h, i],
                        sems.at[len(copies)],
                    )
                    copy.start()
                    copies.append(copy)
    for copy in copies:
        copy.wait()


def pack_cache(cache_keys, cache_values, count):
    convs, slots, span, width = cache_keys.shape
    pairs = convs * width // HEAD
    return pl.pallas_call(
        pack_cache_kernel,
        in_specs=[HBM, HBM],
        out_specs=[VMEM] * count,
        out_shape=[jax.ShapeDtypeStruct((pairs, 2, slots // count, span, HEAD), BF16)] * count,
        scratch_shapes=[pltpu.SemaphoreType.DMA((2 * pairs * count,))],
        compiler_params=pltpu.CompilerParams(vmem_limit_bytes=60 * MIB),
        name="pack_cache",
    )(cache_keys, cache_values)


def prepare_kernel(first_slot, cycle, place, lengths, slots_ref, kv, *refs):
    rest, keys, sums = refs[:-2], refs[-2], refs[-1]
    sources, _, slots, span, _ = kv.shape
    all_slots = slots_ref.shape[1] // cycle
    z, b = place[0], place[1]
    conv = b // (COLUMNS // 2)
    length = lengths[conv]
    rotation = slots_ref[conv, 0] // all_slots
    cached = sources * slots * span

    def base(source, slot):
        member = z * COLUMNS + source
        return (slot * cycle + lax.rem(member - rotation + cycle, cycle)) * span

    if rest:
        new_ref, known = rest
        filler = known[0:16, :].astype(F32)[0:1]
    else:
        first = kv[0, 0, 0, 0:16, :].astype(F32)[0:1]
        second = kv[1, 0, 0, 0:16, :].astype(F32)[0:1]
        filler = jnp.where(base(0, 0) < length, first, second)
    for source in range(sources):
        for slot in range(slots):
            left = length - base(source, first_slot + slot)
            start = (source * slots + slot) * span
            at = slice(start, start + span)
            rows = lax.broadcasted_iota(I32, (span, HEAD), 0) < left
            cols = lax.broadcasted_iota(I32, (HEAD, span), 1) < left
            keys[at, :] = jnp.where(rows, kv[source, 0, slot].astype(F32), filler).astype(BF16)
            turned = kv[source, 1, slot].T.astype(F32)
            sums[0:HEAD, at] = jnp.where(cols, turned, 0.0).astype(BF16)
            sums[HEAD:, at] = jnp.where(cols[:EXTRA], 1.0, 0.0).astype(BF16)
    if rest:
        turn_part = new_ref.shape[0] // 2
        keys[cached:, :] = new_ref[0:turn_part, :]
        sums[0:HEAD, cached:] = new_ref[turn_part:, :].T
        sums[HEAD:, cached:] = jnp.ones((EXTRA, turn_part), BF16)


def prepare(place, lengths, span_slots, first_slot, kv, cycle, new=None, known=None):
    positions = kv.shape[0] * kv.shape[2] * kv.shape[3]
    rest = []
    if new is not None:
        positions += new.shape[0] // 2
        rest = [new, known]
    return pl.pallas_call(
        functools.partial(prepare_kernel, first_slot, cycle),
        in_specs=[SMEM] * 3 + [VMEM] * (1 + len(rest)),
        out_specs=[VMEM] * 2,
        out_shape=[
            jax.ShapeDtypeStruct((positions, HEAD), BF16),
            jax.ShapeDtypeStruct((HEAD + EXTRA, positions), BF16),
        ],
        compiler_params=pltpu.CompilerParams(vmem_limit_bytes=12 * MIB),
        name="prepare",
    )(place, lengths, span_slots, kv, *rest)


def level_of(part):
    coded = part[HEAD:].astype(F32)
    return coded[0:1] + coded[1:2] + coded[2:3]


def combine(parts):
    levels = [level_of(part) for part in parts]
    top = functools.reduce(jnp.maximum, levels)
    shares = [jnp.exp2(level - top) for level in levels]
    total = functools.reduce(jnp.add, shares)
    sums = functools.reduce(
        jnp.add, [part[:HEAD].astype(F32) * share for part, share in zip(parts, shares)]
    )
    return sums, total, top


def attend_kernel(parts, distances, cuts, inits, with_new, *refs):
    count = len(distances)
    place, refs = refs[0], refs[1:]
    q_refs = []
    for pieces in cuts:
        q_refs.append(refs[:pieces])
        refs = refs[pieces:]
    picks = [pick for init in inits for pick in init]
    init_refs, refs = refs[: len(picks)], refs[len(picks) :]
    init_refs = [ref if pick is None else ref.at[pick] for ref, pick in zip(init_refs, picks)]
    keys, sums, outs = refs[0], refs[1], refs[2:]
    if len(outs[0].shape) == 3:
        outs = [outs[0].at[c] for c in range(count)]
    width = outs[0].shape[1]
    columns = count * width
    turn_part = width // 8
    cached = keys.shape[0] - with_new * turn_part
    z = place[0]

    q = [jnp.concatenate([ref[:, 0:width] for ref in held], axis=0) for held in q_refs]
    q = jnp.concatenate(q, axis=1).astype(F32) * SCALE
    high = q.astype(BF16)
    low = (q - high.astype(F32)).astype(BF16)
    q = jnp.concatenate([high, low], axis=0)
    tops, totals, at_init = [], [], 0
    for given in inits:
        if given:
            held, weight, level = combine(init_refs[at_init : at_init + len(given)])
            at_init += len(given)
            tops.append(level)
            totals.append(
                jnp.concatenate([held, jnp.broadcast_to(weight, (EXTRA, width))], axis=0)
            )
        else:
            tops.append(jnp.full((1, width), LOWEST, F32))
            totals.append(jnp.zeros((HEAD + EXTRA, width), F32))
    top = jnp.concatenate(tops, axis=1)
    total = jnp.concatenate(totals, axis=1)
    tiles = [slice(j, j + TILE) for j in range(0, cached, TILE)]
    if with_new:
        tiles.append(slice(cached, cached + turn_part))

    def scores_of(at):
        twice = jnp.concatenate([keys[at, :]] * 2, axis=1)
        scores = dot(twice, q)
        if at.start < cached:
            return scores
        row = lax.broadcasted_iota(I32, (turn_part, width), 0)
        lane = lax.broadcasted_iota(I32, (turn_part, width), 1)
        token = (lane // 64) * 8 + lax.rem(lane, 8)
        ahead = jnp.concatenate(
            [row - token + (z - lax.rem(z + d, parts)) * turn_part for d in distances], axis=1
        )
        return jnp.where(ahead <= 0, scores, LOWEST)

    scores = scores_of(tiles[0])
    for n, at in enumerate(tiles):
        following = scores_of(tiles[n + 1]) if n + 1 < len(tiles) else None
        higher = jnp.maximum(top, jnp.max(scores, axis=0, keepdims=True))
        weights = jnp.exp2(scores - higher).astype(BF16)
        total = total * jnp.exp2(top - higher) + dot(sums[:, at], weights)
        top, scores = higher, following
    denominator = total[HEAD : HEAD + 1]
    out = (total[:HEAD] * (1.0 / denominator)).astype(BF16)
    level = top + jnp.log2(denominator)
    first = level.astype(BF16).astype(F32)
    second = (level - first).astype(BF16).astype(F32)
    third = level - first - second
    row = lax.broadcasted_iota(I32, (EXTRA, columns), 0)
    coded = jnp.where(row == 0, first, jnp.where(row == 1, second, third)).astype(BF16)
    for c in range(count):
        at = slice(c * width, (c + 1) * width)
        outs[c][0:HEAD] = out[:, at]
        outs[c][HEAD:] = coded[:, at]


def attend(place, kv, chunks, distances, inits, parts, with_new, joined):
    keys, sums = kv
    count = len(distances)
    width = chunks[0][0].shape[1] - HEAD
    pieces = [piece for chunk in chunks for piece in chunk]
    cuts = [len(chunk) for chunk in chunks]
    given = [part[0] for init in inits for part in init]
    shape = jax.ShapeDtypeStruct((count,) * joined + (HEAD + EXTRA, width), BF16)
    picks = [[part[1] if len(part) > 1 else None for part in init] for init in inits]
    return pl.pallas_call(
        functools.partial(attend_kernel, parts, distances, cuts, picks, with_new),
        in_specs=[SMEM] + [VMEM] * (len(pieces) + len(given) + 2),
        out_specs=VMEM if joined else [VMEM] * count,
        out_shape=shape if joined else [shape] * count,
        compiler_params=pltpu.CompilerParams(vmem_limit_bytes=16 * MIB),
        cost_estimate=pl.CostEstimate(
            flops=8 * HEAD * count * width * keys.shape[0],
            bytes_accessed=3 * MIB,
            transcendentals=count * width * keys.shape[0],
        ),
        name="attend",
    )(place, *pieces, *given, keys, sums)


def merge_kernel(*refs):
    parts, window_ref, out_ref = refs[:-2], refs[-2], refs[-1]
    sums, total, _ = combine(parts)
    turned = (sums * (1.0 / total)).astype(BF16).T
    columns, rows, _ = out_ref.shape
    rows -= window_ref.shape[1]
    for s in range(columns):
        out_ref[s, 0:rows] = turned[s * rows : (s + 1) * rows]
        out_ref[s, rows:] = window_ref[s]


def merge(parts, windows):
    width = parts[0].shape[1]
    rows = width // COLUMNS + windows.shape[1]
    return pl.pallas_call(
        merge_kernel,
        in_specs=[VMEM] * (len(parts) + 1),
        out_specs=VMEM,
        out_shape=jax.ShapeDtypeStruct((COLUMNS, rows, HEAD), BF16),
        compiler_params=pltpu.CompilerParams(vmem_limit_bytes=8 * MIB),
        name="merge",
    )(*parts, windows)


def turn_slot(length, rotation, member, slots, cycle, span):
    j = lax.rem(member - rotation + cycle, cycle)
    slot = jnp.clip((length // span - j + cycle - 1) // cycle, 0, slots - 1)
    return slot, (j + slot * cycle) * span - length


def windows_kernel(slots, span, cycle, place, lengths, slots_ref, *refs):
    news, out_ref, rows = refs[:-2], refs[-2], refs[-1]
    turn_part = HEAD // 2
    chunks, at = [], 0
    while at < len(news):
        if news[at].shape[0] > turn_part:
            chunks.append((news[at].at[0:turn_part], news[at].at[turn_part:]))
            at += 1
        else:
            chunks.append((news[at], news[at + 1]))
            at += 2
    parts = len(chunks)
    width = news[0].shape[1] - HEAD
    turn = parts * turn_part
    z, b = place[0], place[1]
    conv = b // (COLUMNS // 2)
    rotation = slots_ref[conv, 0] // slots
    edge = jnp.zeros((span, 2 * HEAD), F32)
    rows[0:span] = edge
    rows[span + turn : turn + 2 * span] = edge
    rows[turn + 2 * span :] = edge[0:8]
    for d, chunk in enumerate(chunks):
        start = pl.multiple_of(span + lax.rem(z + d, parts) * turn_part, turn_part)
        rows[pl.ds(start, turn_part), 0:HEAD] = chunk[0][:, width:].astype(F32)
        rows[pl.ds(start, turn_part), HEAD:] = chunk[1][:, width:].astype(F32)
    for to in range(COLUMNS):
        _, token = turn_slot(lengths[conv], rotation, z * COLUMNS + to, slots, cycle, span)
        start = jnp.clip(token + span, 0, turn + span)
        whole = pl.multiple_of(start // 8 * 8, 8)
        window = rows[pl.ds(whole, span + 8), :]
        window = pltpu.roll(window, lax.rem(span + 8 + whole - start, span + 8), 0)
        window = window[0:span].astype(BF16)
        out_ref[to, 0:span] = window[:, 0:HEAD]
        out_ref[to, span:] = window[:, HEAD:]


def windows(place, lengths, span_slots, chunks, slots, span, cycle):
    turn = len(chunks) * HEAD // 2
    pieces = [piece for chunk in chunks for piece in chunk]
    return pl.pallas_call(
        functools.partial(windows_kernel, slots, span, cycle),
        in_specs=[SMEM] * 3 + [VMEM] * len(pieces),
        out_specs=VMEM,
        out_shape=jax.ShapeDtypeStruct((COLUMNS, 2 * span, HEAD), BF16),
        scratch_shapes=[pltpu.VMEM((turn + 2 * span + 8, 2 * HEAD), F32)],
        compiler_params=pltpu.CompilerParams(vmem_limit_bytes=8 * MIB),
        name="windows",
    )(place, lengths, span_slots, *pieces)


def finish_kernel(
    turn, cycle, place, lengths, slots_ref, new_ref, k_ref, v_ref, out_ref, ko_ref, vo_ref
):
    conv = pl.program_id(0)
    _, slots, span, width = k_ref.shape
    heads = width // HEAD
    _, tokens, query_width = out_ref.shape
    group = query_width // width
    done = tokens * group
    for h in range(heads):
        for g in range(group):
            at = (h * group + g) * HEAD
            out_ref[0, :, at : at + HEAD] = new_ref[h, g * tokens : (g + 1) * tokens]
    member = place[0] * COLUMNS + place[1]
    rotation = slots_ref[conv, 0] // slots
    slot, token = turn_slot(lengths[conv], rotation, member, slots, cycle, span)
    ko_ref[...] = k_ref[...]
    vo_ref[...] = v_ref[...]

    @pl.when((token > -span) & (token < turn))
    def _():
        row = lax.broadcasted_iota(I32, (span, HEAD), 0) + token
        inside = (row >= 0) & (row < turn)
        for h in range(heads):
            lanes = slice(h * HEAD, (h + 1) * HEAD)
            for i, (old, out) in enumerate(((k_ref, ko_ref), (v_ref, vo_ref))):
                start = done + i * span
                new = new_ref[h, start : start + span].astype(F32)
                kept = old[0, slot, :, lanes].astype(F32)
                out[0, slot, :, lanes] = jnp.where(inside, new, kept).astype(BF16)


def finish(place, lengths, span_slots, rows, cache_keys, cache_values, queries, turn, cycle):
    convs, slots, span, width = cache_keys.shape
    _, tokens, query_width = queries.shape
    spec = pl.BlockSpec((1, slots, span, width), lambda c: (c, 0, 0, 0))
    block = (rows.shape[0] // convs,) + rows.shape[1:]
    shape = jax.ShapeDtypeStruct(cache_keys.shape, BF16)
    return pl.pallas_call(
        functools.partial(finish_kernel, turn, cycle),
        grid=(convs,),
        in_specs=[SMEM] * 3 + [pl.BlockSpec(block, lambda c: (c, 0, 0)), spec, spec],
        out_specs=[pl.BlockSpec((1, tokens, query_width), lambda c: (c, 0, 0)), spec, spec],
        out_shape=[jax.ShapeDtypeStruct(queries.shape, BF16), shape, shape],
        compiler_params=pltpu.CompilerParams(vmem_limit_bytes=12 * MIB),
        cost_estimate=pl.CostEstimate(flops=0, bytes_accessed=5 * MIB, transcendentals=0),
        name="finish",
    )(place, lengths, span_slots, rows, cache_keys, cache_values)


def on_device(parts, queries, new_keys, new_values, cache_keys, cache_values, lengths, span_slots):
    _, slots, span, _ = cache_keys.shape
    cycle = parts * COLUMNS
    place = jnp.stack([lax.axis_index("z"), lax.axis_index("b")]).astype(I32)
    tie = lax.optimization_barrier

    turn_rows = pack_turn(queries, new_keys, new_values)
    turn_rows, cache_k, cache_v = tie((turn_rows, cache_keys, cache_values))
    turn_rows = lax.all_to_all(turn_rows, "b", 0, 0, tiled=True)
    first, second = pack_cache(cache_k, cache_v, 2)
    turn_rows, first, second = tie((turn_rows, first, second))
    first = lax.all_to_all(first, "b", 0, 0, tiled=True)

    message, new = ring_message(turn_rows)
    chunks = [None] * parts
    chunks[0] = message
    half = message.shape[0] // 2
    far = None

    def run(kv, distances, inits=None, after=(), joined=True):
        held = [c if isinstance(c, tuple) else (c,) for c in (chunks[d] for d in distances)]
        if after:
            held, _ = tie((held, after))
        inits = inits or [()] * len(distances)
        return attend(place, kv, held, distances, inits, parts, kv is far, joined)

    chunks[7], chunks[1] = shift(message, 1), shift(message, -1)
    chunks[6], chunks[2] = shift(chunks[7], 1), shift(chunks[1], -1)
    near = prepare(place, lengths, span_slots, 0, first, cycle)
    n017 = run(near, (0, 1, 7))
    second, chunks[6], chunks[2], n017 = tie((second, chunks[6], chunks[2], n017))
    second = lax.all_to_all(second, "b", 0, 0, tiled=True)
    chunks[5], chunks[3] = shift(chunks[6], 1), shift(chunks[2], -1)
    below, above = shift(chunks[5][:half], 1), shift(chunks[3][half:], -1)
    n35 = run(near, (3, 5))
    below, above, n35, second = tie((below, above, n35, second))
    far = prepare(place, lengths, span_slots, slots // 2, second, cycle, new, near[0])
    chunks[4] = (below, above)
    n4 = run(near, (4,))

    ups = run(far, (4, 3), (((n4, 0),), ((n35, 0),)))
    down3, own = run(far, (5, 0), (((n35, 1),), ((n017, 0),)), (ups,), False)
    ups = shift(ups, 2)
    n26 = run(near, (2, 6), after=(down3,))
    down3 = shift(down3, -2)
    up2, down2 = run(far, (2, 6), (((n26, 0), (ups, 0)), ((n26, 1),)), joined=False)
    up1, down1 = run(
        far, (1, 7), (((n017, 1), (ups, 1)), ((n017, 2), (down3,))), (up2,), False
    )
    up2, down2 = shift(up2, 2), shift(down2, -2)
    seen = [c if isinstance(c, tuple) else (c,) for c in chunks]
    seen, _ = tie((seen, up1))
    rows = windows(place, lengths, span_slots, seen, slots, span, cycle)
    up1, down1 = shift(up1, 1), shift(down1, -1)
    rows = merge([own, up2, down2, up1, down1], rows)
    rows = lax.all_to_all(rows, "b", 0, 0, tiled=True)
    return finish(
        place,
        lengths,
        span_slots,
        rows,
        cache_keys,
        cache_values,
        queries,
        parts * HEAD // 2,
        cycle,
    )


def solution(mesh):
    members, heads, convs = mesh.devices.shape
    parts = members // COLUMNS
    grid = Mesh(mesh.devices.reshape(parts, COLUMNS, heads, convs), ("z", "b", "head", "conv"))
    ctx = ("z", "b")
    turn = P("conv", ctx, "head")
    cache = P("conv", ctx, None, "head")
    return jax.shard_map(
        functools.partial(on_device, parts),
        mesh=grid,
        in_specs=(turn, turn, turn, cache, cache, P("conv"), P("conv", None)),
        out_specs=(turn, cache, cache),
        check_vma=False,
    )
```

```python
import functools
import math

import jax
import jax.numpy as jnp
from jax import lax
from jax.experimental import pallas as pl
from jax.experimental.pallas import tpu as pltpu
from jax.sharding import Mesh, PartitionSpec as P

HEAD = 128
LOWEST = -1e30
SCALE = math.log2(math.e) / math.sqrt(HEAD)
F32, BF16, I32 = jnp.float32, jnp.bfloat16, jnp.int32
MIB = 2**20
EXTRA = 16
TILE = 512
COLUMNS = 8
SMEM = pl.BlockSpec(memory_space=pltpu.SMEM)
VMEM = pl.BlockSpec(memory_space=pltpu.VMEM)
ANY = pl.BlockSpec(memory_space=pl.ANY)
HBM = pl.BlockSpec(memory_space=pltpu.HBM)

def dot(a, b):
    return jnp.dot(a, b, preferred_element_type=F32)


def shift(a, by, size=8):
    return lax.ppermute(a, "z", [(i, (i + by) % size) for i in range(size)])


def pack_turn_kernel(*refs):
    sources, out_ref, held, sems = refs[:3], refs[3], refs[4:7], refs[7]
    copies = [
        pltpu.make_async_copy(source, target, sems.at[i])
        for i, (source, target) in enumerate(zip(sources, held))
    ]
    for copy in copies:
        copy.start()
    for copy in copies:
        copy.wait()
    q_ref, k_ref, v_ref = held
    convs, tokens, width = q_ref.shape
    heads = k_ref.shape[2] // HEAD
    group = width // (heads * HEAD)
    for c in range(convs):
        for h in range(heads):
            pieces = []
            for g in range(group):
                at = (h * group + g) * HEAD
                pieces.append(q_ref[c, :, at : at + HEAD])
            pieces.append(k_ref[c, :, h * HEAD : (h + 1) * HEAD])
            pieces.append(v_ref[c, :, h * HEAD : (h + 1) * HEAD])
            pieces = [piece.astype(F32) for piece in pieces]
            out_ref[c * heads + h] = jnp.concatenate(pieces, axis=0).astype(BF16)


def pack_turn(queries, new_keys, new_values):
    convs, tokens, width = queries.shape
    heads = new_keys.shape[2] // HEAD
    rows = tokens * (width // (heads * HEAD) + 2)
    return pl.pallas_call(
        pack_turn_kernel,
        in_specs=[HBM] * 3,
        out_specs=VMEM,
        out_shape=jax.ShapeDtypeStruct((convs * heads, rows, HEAD), BF16),
        scratch_shapes=[pltpu.VMEM(x.shape, BF16) for x in (queries, new_keys, new_values)]
        + [pltpu.SemaphoreType.DMA((3,))],
        compiler_params=pltpu.CompilerParams(vmem_limit_bytes=60 * MIB),
        name="pack_turn",
    )(queries, new_keys, new_values)


def ring_message_kernel(rows_ref, out_ref, new_ref):
    columns, count, _ = rows_ref.shape
    tokens = 8
    q_rows = count - 2 * tokens
    q = jnp.concatenate([rows_ref[s, 0:q_rows] for s in range(columns)], axis=0)
    news = [rows_ref[s, q_rows:].astype(F32) for s in range(columns)]
    new = [held[:tokens] for held in news] + [held[tokens:] for held in news]
    new = jnp.concatenate(new, axis=0).astype(BF16)
    out_ref[:, 0 : columns * q_rows] = q.T
    out_ref[:, columns * q_rows :] = new
    new_ref[...] = new


def ring_message(rows):
    columns, count, _ = rows.shape
    width = columns * (count - 16)
    return pl.pallas_call(
        ring_message_kernel,
        in_specs=[VMEM],
        out_specs=[VMEM, VMEM],
        out_shape=[
            jax.ShapeDtypeStruct((HEAD, width + HEAD), BF16),
            jax.ShapeDtypeStruct((HEAD, HEAD), BF16),
        ],
        compiler_params=pltpu.CompilerParams(vmem_limit_bytes=6 * MIB),
        name="ring_message",
    )(rows)


def pack_cache_kernel(keys_ref, values_ref, *rest):
    outs, sems = rest[:-1], rest[-1]
    convs, _, _, width = keys_ref.shape
    heads = width // HEAD
    copies = []
    for c in range(convs):
        for h in range(heads):
            for i, ref in enumerate((keys_ref, values_ref)):
                at = 0
                for out in outs:
                    copy = pltpu.make_async_copy(
                        ref.at[c, pl.ds(at, out.shape[2]), :, pl.ds(h * HEAD, HEAD)],
                        out.at[c * heads + h, i],
                        sems.at[len(copies)],
                    )
                    copy.start()
                    copies.append(copy)
                    at += out.shape[2]
    for copy in copies:
        copy.wait()


def pack_cache(cache_keys, cache_values, counts):
    convs, _, span, width = cache_keys.shape
    pairs = convs * width // HEAD
    return pl.pallas_call(
        pack_cache_kernel,
        in_specs=[HBM, HBM],
        out_specs=[VMEM] * len(counts),
        out_shape=[jax.ShapeDtypeStruct((pairs, 2, count, span, HEAD), BF16) for count in counts],
        scratch_shapes=[pltpu.SemaphoreType.DMA((2 * pairs * len(counts),))],
        compiler_params=pltpu.CompilerParams(vmem_limit_bytes=60 * MIB),
        name="pack_cache",
    )(cache_keys, cache_values)


def prepare_kernel(first_slot, cycle, place, lengths, slots_ref, kv, *refs):
    rest, keys, sums = refs[:-2], refs[-2], refs[-1]
    sources, _, slots, span, _ = kv.shape
    all_slots = slots_ref.shape[1] // cycle
    z, b = place[0], place[1]
    conv = b // (COLUMNS // 2)
    length = lengths[conv]
    rotation = slots_ref[conv, 0] // all_slots
    cached = sources * slots * span

    def base(source, slot):
        member = z * COLUMNS + source
        return (slot * cycle + lax.rem(member - rotation + cycle, cycle)) * span

    if rest:
        new_ref, known = rest
        filler = known[0:16, :].astype(F32)[0:1]
    else:
        first = kv[0, 0, 0, 0:16, :].astype(F32)[0:1]
        second = kv[1, 0, 0, 0:16, :].astype(F32)[0:1]
        filler = jnp.where(base(0, 0) < length, first, second)
    for source in range(sources):
        for slot in range(slots):
            left = length - base(source, first_slot + slot)
            start = (source * slots + slot) * span
            at = slice(start, start + span)
            rows = lax.broadcasted_iota(I32, (span, HEAD), 0) < left
            cols = lax.broadcasted_iota(I32, (HEAD, span), 1) < left
            keys[at, :] = jnp.where(rows, kv[source, 0, slot].astype(F32), filler).astype(BF16)
            turned = kv[source, 1, slot].T.astype(F32)
            sums[0:HEAD, at] = jnp.where(cols, turned, 0.0).astype(BF16)
            sums[HEAD:, at] = jnp.where(cols[:EXTRA], 1.0, 0.0).astype(BF16)
    if rest:
        turn_part = new_ref.shape[0] // 2
        keys[cached:, :] = new_ref[0:turn_part, :]
        sums[0:HEAD, cached:] = new_ref[turn_part:, :].T
        sums[HEAD:, cached:] = jnp.ones((EXTRA, turn_part), BF16)


def prepare(place, lengths, span_slots, first_slot, kv, cycle, new=None, known=None):
    positions = kv.shape[0] * kv.shape[2] * kv.shape[3]
    rest = []
    if new is not None:
        positions += new.shape[0] // 2
        rest = [new, known]
    return pl.pallas_call(
        functools.partial(prepare_kernel, first_slot, cycle),
        in_specs=[SMEM] * 3 + [VMEM] * (1 + len(rest)),
        out_specs=[VMEM] * 2,
        out_shape=[
            jax.ShapeDtypeStruct((positions, HEAD), BF16),
            jax.ShapeDtypeStruct((HEAD + EXTRA, positions), BF16),
        ],
        compiler_params=pltpu.CompilerParams(vmem_limit_bytes=12 * MIB),
        name="prepare",
    )(place, lengths, span_slots, kv, *rest)


def level_of(part):
    coded = part[HEAD:].astype(F32)
    return coded[0:1] + coded[1:2] + coded[2:3]


def combine(parts):
    levels = [level_of(part) for part in parts]
    top = functools.reduce(jnp.maximum, levels)
    shares = [jnp.exp2(level - top) for level in levels]
    total = functools.reduce(jnp.add, shares)
    sums = functools.reduce(
        jnp.add, [part[:HEAD].astype(F32) * share for part, share in zip(parts, shares)]
    )
    return sums, total, top


def attend_kernel(parts, distances, cuts, inits, with_new, *refs):
    count = len(distances)
    place, refs = refs[0], refs[1:]
    q_refs = []
    for pieces in cuts:
        q_refs.append(refs[:pieces])
        refs = refs[pieces:]
    picks = [pick for init in inits for pick in init]
    init_refs, refs = refs[: len(picks)], refs[len(picks) :]
    init_refs = [ref if pick is None else ref.at[pick] for ref, pick in zip(init_refs, picks)]
    keys, sums, outs = refs[0], refs[1], refs[2:]
    if len(outs[0].shape) == 3:
        outs = [outs[0].at[c] for c in range(count)]
    width = outs[0].shape[1]
    columns = count * width
    turn_part = width // 8
    cached = keys.shape[0] - with_new * turn_part
    z = place[0]

    q = [jnp.concatenate([ref[:, 0:width] for ref in held], axis=0) for held in q_refs]
    q = jnp.concatenate(q, axis=1).astype(F32) * SCALE
    high = q.astype(BF16)
    low = (q - high.astype(F32)).astype(BF16)
    q = jnp.concatenate([high, low], axis=0)
    tops, totals, at_init = [], [], 0
    for given in inits:
        if given:
            held, weight, level = combine(init_refs[at_init : at_init + len(given)])
            at_init += len(given)
            tops.append(level)
            totals.append(
                jnp.concatenate([held, jnp.broadcast_to(weight, (EXTRA, width))], axis=0)
            )
        else:
            tops.append(jnp.full((1, width), LOWEST, F32))
            totals.append(jnp.zeros((HEAD + EXTRA, width), F32))
    top = jnp.concatenate(tops, axis=1)
    total = jnp.concatenate(totals, axis=1)
    tiles = [slice(j, j + TILE) for j in range(0, cached, TILE)]
    if with_new:
        tiles.append(slice(cached, cached + turn_part))

    def scores_of(at):
        twice = jnp.concatenate([keys[at, :]] * 2, axis=1)
        scores = dot(twice, q)
        if at.start < cached:
            return scores
        row = lax.broadcasted_iota(I32, (turn_part, width), 0)
        lane = lax.broadcasted_iota(I32, (turn_part, width), 1)
        token = (lane // 64) * 8 + lax.rem(lane, 8)
        ahead = jnp.concatenate(
            [row - token + (z - lax.rem(z + d, parts)) * turn_part for d in distances], axis=1
        )
        return jnp.where(ahead <= 0, scores, LOWEST)

    scores = scores_of(tiles[0])
    for n, at in enumerate(tiles):
        following = scores_of(tiles[n + 1]) if n + 1 < len(tiles) else None
        higher = jnp.maximum(top, jnp.max(scores, axis=0, keepdims=True))
        weights = jnp.exp2(scores - higher).astype(BF16)
        total = total * jnp.exp2(top - higher) + dot(sums[:, at], weights)
        top, scores = higher, following
    denominator = total[HEAD : HEAD + 1]
    out = (total[:HEAD] * (1.0 / denominator)).astype(BF16)
    level = top + jnp.log2(denominator)
    first = level.astype(BF16).astype(F32)
    second = (level - first).astype(BF16).astype(F32)
    third = level - first - second
    row = lax.broadcasted_iota(I32, (EXTRA, columns), 0)
    coded = jnp.where(row == 0, first, jnp.where(row == 1, second, third)).astype(BF16)
    for c in range(count):
        at = slice(c * width, (c + 1) * width)
        outs[c][0:HEAD] = out[:, at]
        outs[c][HEAD:] = coded[:, at]


def attend(place, kv, chunks, distances, inits, parts, with_new, joined):
    keys, sums = kv
    count = len(distances)
    width = chunks[0][0].shape[1] - HEAD
    pieces = [piece for chunk in chunks for piece in chunk]
    cuts = [len(chunk) for chunk in chunks]
    given = [part[0] for init in inits for part in init]
    shape = jax.ShapeDtypeStruct((count,) * joined + (HEAD + EXTRA, width), BF16)
    picks = [[part[1] if len(part) > 1 else None for part in init] for init in inits]
    return pl.pallas_call(
        functools.partial(attend_kernel, parts, distances, cuts, picks, with_new),
        in_specs=[SMEM] + [VMEM] * (len(pieces) + len(given) + 2),
        out_specs=VMEM if joined else [VMEM] * count,
        out_shape=shape if joined else [shape] * count,
        compiler_params=pltpu.CompilerParams(vmem_limit_bytes=16 * MIB),
        cost_estimate=pl.CostEstimate(
            flops=8 * HEAD * count * width * keys.shape[0],
            bytes_accessed=3 * MIB,
            transcendentals=count * width * keys.shape[0],
        ),
        name="attend",
    )(place, *pieces, *given, keys, sums)


def merge_kernel(*refs):
    parts, window_ref, out_ref = refs[:-2], refs[-2], refs[-1]
    sums, total, _ = combine(parts)
    turned = (sums * (1.0 / total)).astype(BF16).T
    columns, rows, _ = out_ref.shape
    rows -= window_ref.shape[1]
    for s in range(columns):
        out_ref[s, 0:rows] = turned[s * rows : (s + 1) * rows]
        out_ref[s, rows:] = window_ref[s]


def merge(parts, windows):
    width = parts[0].shape[1]
    rows = width // COLUMNS + windows.shape[1]
    return pl.pallas_call(
        merge_kernel,
        in_specs=[VMEM] * (len(parts) + 1),
        out_specs=VMEM,
        out_shape=jax.ShapeDtypeStruct((COLUMNS, rows, HEAD), BF16),
        compiler_params=pltpu.CompilerParams(vmem_limit_bytes=8 * MIB),
        name="merge",
    )(*parts, windows)


def turn_slot(length, rotation, member, slots, cycle, span):
    j = lax.rem(member - rotation + cycle, cycle)
    slot = jnp.clip((length // span - j + cycle - 1) // cycle, 0, slots - 1)
    return slot, (j + slot * cycle) * span - length


def windows_kernel(slots, span, cycle, place, lengths, slots_ref, *refs):
    news, out_ref, rows = refs[:-2], refs[-2], refs[-1]
    turn_part = HEAD // 2
    chunks, at = [], 0
    while at < len(news):
        if news[at].shape[0] > turn_part:
            chunks.append((news[at].at[0:turn_part], news[at].at[turn_part:]))
            at += 1
        else:
            chunks.append((news[at], news[at + 1]))
            at += 2
    parts = len(chunks)
    width = news[0].shape[1] - HEAD
    turn = parts * turn_part
    z, b = place[0], place[1]
    conv = b // (COLUMNS // 2)
    rotation = slots_ref[conv, 0] // slots
    edge = jnp.zeros((span, 2 * HEAD), F32)
    rows[0:span] = edge
    rows[span + turn : turn + 2 * span] = edge
    rows[turn + 2 * span :] = edge[0:8]
    for d, chunk in enumerate(chunks):
        start = pl.multiple_of(span + lax.rem(z + d, parts) * turn_part, turn_part)
        rows[pl.ds(start, turn_part), 0:HEAD] = chunk[0][:, width:].astype(F32)
        rows[pl.ds(start, turn_part), HEAD:] = chunk[1][:, width:].astype(F32)
    for to in range(COLUMNS):
        _, token = turn_slot(lengths[conv], rotation, z * COLUMNS + to, slots, cycle, span)
        start = jnp.clip(token + span, 0, turn + span)
        whole = pl.multiple_of(start // 8 * 8, 8)
        window = rows[pl.ds(whole, span + 8), :]
        window = pltpu.roll(window, lax.rem(span + 8 + whole - start, span + 8), 0)
        window = window[0:span].astype(BF16)
        out_ref[to, 0:span] = window[:, 0:HEAD]
        out_ref[to, span:] = window[:, HEAD:]


def windows(place, lengths, span_slots, chunks, slots, span, cycle):
    turn = len(chunks) * HEAD // 2
    pieces = [piece for chunk in chunks for piece in chunk]
    return pl.pallas_call(
        functools.partial(windows_kernel, slots, span, cycle),
        in_specs=[SMEM] * 3 + [VMEM] * len(pieces),
        out_specs=VMEM,
        out_shape=jax.ShapeDtypeStruct((COLUMNS, 2 * span, HEAD), BF16),
        scratch_shapes=[pltpu.VMEM((turn + 2 * span + 8, 2 * HEAD), F32)],
        compiler_params=pltpu.CompilerParams(vmem_limit_bytes=8 * MIB),
        name="windows",
    )(place, lengths, span_slots, *pieces)


def finish_kernel(
    turn, cycle, place, lengths, slots_ref, new_ref, k_ref, v_ref, out_ref, ko_ref, vo_ref
):
    conv = pl.program_id(0)
    _, slots, span, width = k_ref.shape
    heads = width // HEAD
    _, tokens, query_width = out_ref.shape
    group = query_width // width
    done = tokens * group
    for h in range(heads):
        held = new_ref[h, 0:done].astype(F32)
        for g in range(group):
            at = (h * group + g) * HEAD
            out_ref[0, :, at : at + HEAD] = held[g * tokens : (g + 1) * tokens].astype(BF16)
    member = place[0] * COLUMNS + place[1]
    rotation = slots_ref[conv, 0] // slots
    slot, token = turn_slot(lengths[conv], rotation, member, slots, cycle, span)
    ko_ref[...] = k_ref[...]
    vo_ref[...] = v_ref[...]

    @pl.when((token > -span) & (token < turn))
    def _():
        row = lax.broadcasted_iota(I32, (span, HEAD), 0) + token
        inside = (row >= 0) & (row < turn)
        for h in range(heads):
            lanes = slice(h * HEAD, (h + 1) * HEAD)
            for i, (old, out) in enumerate(((k_ref, ko_ref), (v_ref, vo_ref))):
                start = done + i * span
                new = new_ref[h, start : start + span].astype(F32)
                kept = old[0, slot, :, lanes].astype(F32)
                out[0, slot, :, lanes] = jnp.where(inside, new, kept).astype(BF16)


def finish(place, lengths, span_slots, rows, cache_keys, cache_values, queries, turn, cycle):
    convs, slots, span, width = cache_keys.shape
    _, tokens, query_width = queries.shape
    spec = pl.BlockSpec((1, slots, span, width), lambda c: (c, 0, 0, 0))
    block = (rows.shape[0] // convs,) + rows.shape[1:]
    shape = jax.ShapeDtypeStruct(cache_keys.shape, BF16)
    return pl.pallas_call(
        functools.partial(finish_kernel, turn, cycle),
        grid=(convs,),
        in_specs=[SMEM] * 3 + [pl.BlockSpec(block, lambda c: (c, 0, 0)), spec, spec],
        out_specs=[pl.BlockSpec((1, tokens, query_width), lambda c: (c, 0, 0)), spec, spec],
        out_shape=[jax.ShapeDtypeStruct(queries.shape, BF16), shape, shape],
        compiler_params=pltpu.CompilerParams(vmem_limit_bytes=12 * MIB),
        cost_estimate=pl.CostEstimate(flops=0, bytes_accessed=5 * MIB, transcendentals=0),
        name="finish",
    )(place, lengths, span_slots, rows, cache_keys, cache_values)


def on_device(parts, queries, new_keys, new_values, cache_keys, cache_values, lengths, span_slots):
    _, slots, span, _ = cache_keys.shape
    cycle = parts * COLUMNS
    place = jnp.stack([lax.axis_index("z"), lax.axis_index("b")]).astype(I32)
    tie = lax.optimization_barrier

    turn_rows = pack_turn(queries, new_keys, new_values)
    turn_rows, cache_k, cache_v = tie((turn_rows, cache_keys, cache_values))
    turn_rows = lax.all_to_all(turn_rows, "b", 0, 0, tiled=True)
    first, second = pack_cache(cache_k, cache_v, (1, slots - 1))
    turn_rows, first, second = tie((turn_rows, first, second))
    first = lax.all_to_all(first, "b", 0, 0, tiled=True)

    message, new = ring_message(turn_rows)
    chunks = [None] * parts
    chunks[0] = message
    half = message.shape[0] // 2
    far = None

    def run(kv, distances, inits=None, after=(), joined=True):
        held = [c if isinstance(c, tuple) else (c,) for c in (chunks[d] for d in distances)]
        if after:
            held, _ = tie((held, after))
        inits = inits or [()] * len(distances)
        return attend(place, kv, held, distances, inits, parts, kv is far, joined)

    chunks[7], chunks[1] = shift(message, 1), shift(message, -1)
    second, chunks[7], chunks[1] = tie((second, chunks[7], chunks[1]))
    second = lax.all_to_all(second, "b", 0, 0, tiled=True)
    chunks[6], chunks[2] = shift(chunks[7], 1), shift(chunks[1], -1)
    near = prepare(place, lengths, span_slots, 0, first, cycle)
    n017 = run(near, (0, 1, 7))
    chunks[6], chunks[2], n017 = tie((chunks[6], chunks[2], n017))
    chunks[5], chunks[3] = shift(chunks[6], 1), shift(chunks[2], -1)
    chunks[4] = (shift(chunks[6][:half], 2), shift(chunks[2][half:], -2))
    n26 = run(near, (2, 6), after=(n017,))
    n435 = run(near, (4, 3, 5), after=(n26,))
    n435, second = tie((n435, second))
    far = prepare(place, lengths, span_slots, 1, second, cycle, new, near[0])

    up4, up3 = run(far, (4, 3), (((n435, 0),), ((n435, 1),)), joined=False)
    down3, own = run(far, (5, 0), (((n435, 2),), ((n017, 0),)), (up4,), False)
    up4, up3 = shift(up4, 2), shift(up3, 2)
    up2, down2 = run(far, (2, 6), (((n26, 0), (up4,)), ((n26, 1),)), (down3,), False)
    down3 = shift(down3, -2)
    up1, down1 = run(
        far, (1, 7), (((n017, 1), (up3,)), ((n017, 2), (down3,))), (up2,), False
    )
    up2, down2 = shift(up2, 2), shift(down2, -2)
    seen = [c if isinstance(c, tuple) else (c,) for c in chunks]
    seen, up2, down2 = tie((seen, up2, down2))
    rows = windows(place, lengths, span_slots, seen, slots, span, cycle)
    up1, down1 = shift(up1, 1), shift(down1, -1)
    rows = merge([own, up2, down2, up1, down1], rows)
    rows = lax.all_to_all(rows, "b", 0, 0, tiled=True)
    return finish(
        place,
        lengths,
        span_slots,
        rows,
        cache_keys,
        cache_values,
        queries,
        parts * HEAD // 2,
        cycle,
    )


def solution(mesh):
    members, heads, convs = mesh.devices.shape
    parts = members // COLUMNS
    grid = Mesh(mesh.devices.reshape(parts, COLUMNS, heads, convs), ("z", "b", "head", "conv"))
    ctx = ("z", "b")
    turn = P("conv", ctx, "head")
    cache = P("conv", ctx, None, "head")
    return jax.shard_map(
        functools.partial(on_device, parts),
        mesh=grid,
        in_specs=(turn, turn, turn, cache, cache, P("conv"), P("conv", None)),
        out_specs=(turn, cache, cache),
        check_vma=False,
    )
```

```python
import functools
import math

import jax
import jax.numpy as jnp
from jax import lax
from jax.experimental import pallas as pl
from jax.experimental.pallas import tpu as pltpu
from jax.sharding import Mesh, PartitionSpec as P

HEAD = 128
LOWEST = -1e30
SCALE = math.log2(math.e) / math.sqrt(HEAD)
F32, BF16, I32 = jnp.float32, jnp.bfloat16, jnp.int32
MIB = 2**20
EXTRA = 16
TILE = 512
COLUMNS = 8
SMEM = pl.BlockSpec(memory_space=pltpu.SMEM)
VMEM = pl.BlockSpec(memory_space=pltpu.VMEM)
ANY = pl.BlockSpec(memory_space=pl.ANY)
HBM = pl.BlockSpec(memory_space=pltpu.HBM)

def dot(a, b):
    return jnp.dot(a, b, preferred_element_type=F32)


def shift(a, by, size=8):
    return lax.ppermute(a, "z", [(i, (i + by) % size) for i in range(size)])


def pack_turn_kernel(*refs):
    sources, out_ref, held, sems = refs[:3], refs[3], refs[4:7], refs[7]
    copies = [
        pltpu.make_async_copy(source, target, sems.at[i])
        for i, (source, target) in enumerate(zip(sources, held))
    ]
    for copy in copies:
        copy.start()
    for copy in copies:
        copy.wait()
    q_ref, k_ref, v_ref = held
    convs, tokens, width = q_ref.shape
    heads = k_ref.shape[2] // HEAD
    group = width // (heads * HEAD)
    for c in range(convs):
        for h in range(heads):
            pieces = []
            for g in range(group):
                at = (h * group + g) * HEAD
                pieces.append(q_ref[c, :, at : at + HEAD])
            pieces.append(k_ref[c, :, h * HEAD : (h + 1) * HEAD])
            pieces.append(v_ref[c, :, h * HEAD : (h + 1) * HEAD])
            pieces = [piece.astype(F32) for piece in pieces]
            out_ref[c * heads + h] = jnp.concatenate(pieces, axis=0).astype(BF16)


def pack_turn(queries, new_keys, new_values):
    convs, tokens, width = queries.shape
    heads = new_keys.shape[2] // HEAD
    rows = tokens * (width // (heads * HEAD) + 2)
    return pl.pallas_call(
        pack_turn_kernel,
        in_specs=[HBM] * 3,
        out_specs=VMEM,
        out_shape=jax.ShapeDtypeStruct((convs * heads, rows, HEAD), BF16),
        scratch_shapes=[pltpu.VMEM(x.shape, BF16) for x in (queries, new_keys, new_values)]
        + [pltpu.SemaphoreType.DMA((3,))],
        compiler_params=pltpu.CompilerParams(vmem_limit_bytes=60 * MIB),
        name="pack_turn",
    )(queries, new_keys, new_values)


def ring_message_kernel(rows_ref, out_ref, new_ref):
    columns, count, _ = rows_ref.shape
    tokens = 8
    q_rows = count - 2 * tokens
    q = jnp.concatenate([rows_ref[s, 0:q_rows] for s in range(columns)], axis=0)
    news = [rows_ref[s, q_rows:].astype(F32) for s in range(columns)]
    new = [held[:tokens] for held in news] + [held[tokens:] for held in news]
    new = jnp.concatenate(new, axis=0).astype(BF16)
    out_ref[:, 0 : columns * q_rows] = q.T
    out_ref[:, columns * q_rows :] = new
    new_ref[...] = new


def ring_message(rows):
    columns, count, _ = rows.shape
    width = columns * (count - 16)
    return pl.pallas_call(
        ring_message_kernel,
        in_specs=[VMEM],
        out_specs=[VMEM, VMEM],
        out_shape=[
            jax.ShapeDtypeStruct((HEAD, width + HEAD), BF16),
            jax.ShapeDtypeStruct((HEAD, HEAD), BF16),
        ],
        compiler_params=pltpu.CompilerParams(vmem_limit_bytes=6 * MIB),
        name="ring_message",
    )(rows)


def pack_cache_kernel(keys_ref, values_ref, *rest):
    outs, sems = rest[:-1], rest[-1]
    convs, _, _, width = keys_ref.shape
    heads = width // HEAD
    copies = []
    for c in range(convs):
        for h in range(heads):
            for i, ref in enumerate((keys_ref, values_ref)):
                at = 0
                for out in outs:
                    copy = pltpu.make_async_copy(
                        ref.at[c, pl.ds(at, out.shape[2]), :, pl.ds(h * HEAD, HEAD)],
                        out.at[c * heads + h, i],
                        sems.at[len(copies)],
                    )
                    copy.start()
                    copies.append(copy)
                    at += out.shape[2]
    for copy in copies:
        copy.wait()


def pack_cache(cache_keys, cache_values, counts):
    convs, _, span, width = cache_keys.shape
    pairs = convs * width // HEAD
    return pl.pallas_call(
        pack_cache_kernel,
        in_specs=[HBM, HBM],
        out_specs=[VMEM] * len(counts),
        out_shape=[jax.ShapeDtypeStruct((pairs, 2, count, span, HEAD), BF16) for count in counts],
        scratch_shapes=[pltpu.SemaphoreType.DMA((2 * pairs * len(counts),))],
        compiler_params=pltpu.CompilerParams(vmem_limit_bytes=60 * MIB),
        name="pack_cache",
    )(cache_keys, cache_values)


def prepare_kernel(first_slot, cycle, place, lengths, slots_ref, kv, *refs):
    rest, keys, sums = refs[:-2], refs[-2], refs[-1]
    sources, _, slots, span, _ = kv.shape
    all_slots = slots_ref.shape[1] // cycle
    z, b = place[0], place[1]
    conv = b // (COLUMNS // 2)
    length = lengths[conv]
    rotation = slots_ref[conv, 0] // all_slots
    cached = sources * slots * span

    def base(source, slot):
        member = z * COLUMNS + source
        return (slot * cycle + lax.rem(member - rotation + cycle, cycle)) * span

    if rest:
        new_ref, known = rest
        filler = known[0:16, :].astype(F32)[0:1]
    else:
        first = kv[0, 0, 0, 0:16, :].astype(F32)[0:1]
        second = kv[1, 0, 0, 0:16, :].astype(F32)[0:1]
        filler = jnp.where(base(0, 0) < length, first, second)
    for source in range(sources):
        for slot in range(slots):
            left = length - base(source, first_slot + slot)
            start = (source * slots + slot) * span
            at = slice(start, start + span)
            rows = lax.broadcasted_iota(I32, (span, HEAD), 0) < left
            cols = lax.broadcasted_iota(I32, (HEAD, span), 1) < left
            keys[at, :] = jnp.where(rows, kv[source, 0, slot].astype(F32), filler).astype(BF16)
            turned = kv[source, 1, slot].T.astype(F32)
            sums[0:HEAD, at] = jnp.where(cols, turned, 0.0).astype(BF16)
            sums[HEAD:, at] = jnp.where(cols[:EXTRA], 1.0, 0.0).astype(BF16)
    if rest:
        turn_part = new_ref.shape[0] // 2
        keys[cached:, :] = new_ref[0:turn_part, :]
        sums[0:HEAD, cached:] = new_ref[turn_part:, :].T
        sums[HEAD:, cached:] = jnp.ones((EXTRA, turn_part), BF16)


def prepare(place, lengths, span_slots, first_slot, kv, cycle, new=None, known=None):
    positions = kv.shape[0] * kv.shape[2] * kv.shape[3]
    rest = []
    if new is not None:
        positions += new.shape[0] // 2
        rest = [new, known]
    return pl.pallas_call(
        functools.partial(prepare_kernel, first_slot, cycle),
        in_specs=[SMEM] * 3 + [VMEM] * (1 + len(rest)),
        out_specs=[VMEM] * 2,
        out_shape=[
            jax.ShapeDtypeStruct((positions, HEAD), BF16),
            jax.ShapeDtypeStruct((HEAD + EXTRA, positions), BF16),
        ],
        compiler_params=pltpu.CompilerParams(vmem_limit_bytes=12 * MIB),
        name="prepare",
    )(place, lengths, span_slots, kv, *rest)


def level_of(part):
    coded = part[HEAD:].astype(F32)
    return coded[0:1] + coded[1:2] + coded[2:3]


def combine(parts):
    levels = [level_of(part) for part in parts]
    top = functools.reduce(jnp.maximum, levels)
    shares = [jnp.exp2(level - top) for level in levels]
    total = functools.reduce(jnp.add, shares)
    sums = functools.reduce(
        jnp.add, [part[:HEAD].astype(F32) * share for part, share in zip(parts, shares)]
    )
    return sums, total, top


def attend_kernel(parts, distances, cuts, inits, with_new, *refs):
    count = len(distances)
    place, refs = refs[0], refs[1:]
    q_refs = []
    for pieces in cuts:
        q_refs.append(refs[:pieces])
        refs = refs[pieces:]
    picks = [pick for init in inits for pick in init]
    init_refs, refs = refs[: len(picks)], refs[len(picks) :]
    init_refs = [ref if pick is None else ref.at[pick] for ref, pick in zip(init_refs, picks)]
    keys, sums, outs = refs[0], refs[1], refs[2:]
    if len(outs[0].shape) == 3:
        outs = [outs[0].at[c] for c in range(count)]
    width = outs[0].shape[1]
    columns = count * width
    turn_part = width // 8
    cached = keys.shape[0] - with_new * turn_part
    z = place[0]

    q = [jnp.concatenate([ref[:, 0:width] for ref in held], axis=0) for held in q_refs]
    q = jnp.concatenate(q, axis=1).astype(F32) * SCALE
    high = q.astype(BF16)
    low = (q - high.astype(F32)).astype(BF16)
    q = jnp.concatenate([high, low], axis=0)
    tops, totals, at_init = [], [], 0
    for given in inits:
        if given:
            held, weight, level = combine(init_refs[at_init : at_init + len(given)])
            at_init += len(given)
            tops.append(level)
            totals.append(
                jnp.concatenate([held, jnp.broadcast_to(weight, (EXTRA, width))], axis=0)
            )
        else:
            tops.append(jnp.full((1, width), LOWEST, F32))
            totals.append(jnp.zeros((HEAD + EXTRA, width), F32))
    top = jnp.concatenate(tops, axis=1)
    total = jnp.concatenate(totals, axis=1)
    tiles = [slice(j, j + TILE) for j in range(0, cached, TILE)]
    if with_new:
        tiles.append(slice(cached, cached + turn_part))

    def scores_of(at):
        twice = jnp.concatenate([keys[at, :]] * 2, axis=1)
        scores = dot(twice, q)
        if at.start < cached:
            return scores
        row = lax.broadcasted_iota(I32, (turn_part, width), 0)
        lane = lax.broadcasted_iota(I32, (turn_part, width), 1)
        token = (lane // 64) * 8 + lax.rem(lane, 8)
        ahead = jnp.concatenate(
            [row - token + (z - lax.rem(z + d, parts)) * turn_part for d in distances], axis=1
        )
        return jnp.where(ahead <= 0, scores, LOWEST)

    scores = scores_of(tiles[0])
    for n, at in enumerate(tiles):
        following = scores_of(tiles[n + 1]) if n + 1 < len(tiles) else None
        higher = jnp.maximum(top, jnp.max(scores, axis=0, keepdims=True))
        weights = jnp.exp2(scores - higher).astype(BF16)
        total = total * jnp.exp2(top - higher) + dot(sums[:, at], weights)
        top, scores = higher, following
    denominator = total[HEAD : HEAD + 1]
    out = (total[:HEAD] * (1.0 / denominator)).astype(BF16)
    level = top + jnp.log2(denominator)
    first = level.astype(BF16).astype(F32)
    second = (level - first).astype(BF16).astype(F32)
    third = level - first - second
    row = lax.broadcasted_iota(I32, (EXTRA, columns), 0)
    coded = jnp.where(row == 0, first, jnp.where(row == 1, second, third)).astype(BF16)
    for c in range(count):
        at = slice(c * width, (c + 1) * width)
        outs[c][0:HEAD] = out[:, at]
        outs[c][HEAD:] = coded[:, at]


def attend(place, kv, chunks, distances, inits, parts, with_new, joined):
    keys, sums = kv
    count = len(distances)
    width = chunks[0][0].shape[1] - HEAD
    pieces = [piece for chunk in chunks for piece in chunk]
    cuts = [len(chunk) for chunk in chunks]
    given = [part[0] for init in inits for part in init]
    shape = jax.ShapeDtypeStruct((count,) * joined + (HEAD + EXTRA, width), BF16)
    picks = [[part[1] if len(part) > 1 else None for part in init] for init in inits]
    return pl.pallas_call(
        functools.partial(attend_kernel, parts, distances, cuts, picks, with_new),
        in_specs=[SMEM] + [VMEM] * (len(pieces) + len(given) + 2),
        out_specs=VMEM if joined else [VMEM] * count,
        out_shape=shape if joined else [shape] * count,
        compiler_params=pltpu.CompilerParams(vmem_limit_bytes=16 * MIB),
        cost_estimate=pl.CostEstimate(
            flops=8 * HEAD * count * width * keys.shape[0],
            bytes_accessed=3 * MIB,
            transcendentals=count * width * keys.shape[0],
        ),
        name="attend",
    )(place, *pieces, *given, keys, sums)


def merge_kernel(*refs):
    parts, window_ref, out_ref = refs[:-2], refs[-2], refs[-1]
    sums, total, _ = combine(parts)
    turned = (sums * (1.0 / total)).astype(BF16).T
    columns, rows, _ = out_ref.shape
    rows -= window_ref.shape[1]
    for s in range(columns):
        out_ref[s, 0:rows] = turned[s * rows : (s + 1) * rows]
        out_ref[s, rows:] = window_ref[s]


def merge(parts, windows):
    width = parts[0].shape[1]
    rows = width // COLUMNS + windows.shape[1]
    return pl.pallas_call(
        merge_kernel,
        in_specs=[VMEM] * (len(parts) + 1),
        out_specs=VMEM,
        out_shape=jax.ShapeDtypeStruct((COLUMNS, rows, HEAD), BF16),
        compiler_params=pltpu.CompilerParams(vmem_limit_bytes=8 * MIB),
        name="merge",
    )(*parts, windows)


def turn_slot(length, rotation, member, slots, cycle, span):
    j = lax.rem(member - rotation + cycle, cycle)
    slot = jnp.clip((length // span - j + cycle - 1) // cycle, 0, slots - 1)
    return slot, (j + slot * cycle) * span - length


def windows_kernel(slots, span, cycle, place, lengths, slots_ref, *refs):
    news, out_ref, rows = refs[:-2], refs[-2], refs[-1]
    turn_part = HEAD // 2
    chunks, at = [], 0
    while at < len(news):
        if news[at].shape[0] > turn_part:
            chunks.append((news[at].at[0:turn_part], news[at].at[turn_part:]))
            at += 1
        else:
            chunks.append((news[at], news[at + 1]))
            at += 2
    parts = len(chunks)
    width = news[0].shape[1] - HEAD
    turn = parts * turn_part
    z, b = place[0], place[1]
    conv = b // (COLUMNS // 2)
    rotation = slots_ref[conv, 0] // slots
    edge = jnp.zeros((span, 2 * HEAD), F32)
    rows[0:span] = edge
    rows[span + turn : turn + 2 * span] = edge
    rows[turn + 2 * span :] = edge[0:8]
    for d, chunk in enumerate(chunks):
        start = pl.multiple_of(span + lax.rem(z + d, parts) * turn_part, turn_part)
        rows[pl.ds(start, turn_part), 0:HEAD] = chunk[0][:, width:].astype(F32)
        rows[pl.ds(start, turn_part), HEAD:] = chunk[1][:, width:].astype(F32)
    for to in range(COLUMNS):
        _, token = turn_slot(lengths[conv], rotation, z * COLUMNS + to, slots, cycle, span)
        start = jnp.clip(token + span, 0, turn + span)
        whole = pl.multiple_of(start // 8 * 8, 8)
        window = rows[pl.ds(whole, span + 8), :]
        window = pltpu.roll(window, lax.rem(span + 8 + whole - start, span + 8), 0)
        window = window[0:span].astype(BF16)
        out_ref[to, 0:span] = window[:, 0:HEAD]
        out_ref[to, span:] = window[:, HEAD:]


def windows(place, lengths, span_slots, chunks, slots, span, cycle):
    turn = len(chunks) * HEAD // 2
    pieces = [piece for chunk in chunks for piece in chunk]
    return pl.pallas_call(
        functools.partial(windows_kernel, slots, span, cycle),
        in_specs=[SMEM] * 3 + [VMEM] * len(pieces),
        out_specs=VMEM,
        out_shape=jax.ShapeDtypeStruct((COLUMNS, 2 * span, HEAD), BF16),
        scratch_shapes=[pltpu.VMEM((turn + 2 * span + 8, 2 * HEAD), F32)],
        compiler_params=pltpu.CompilerParams(vmem_limit_bytes=8 * MIB),
        name="windows",
    )(place, lengths, span_slots, *pieces)


def finish_kernel(
    turn, cycle, place, lengths, slots_ref, new_ref, k_ref, v_ref, out_ref, ko_ref, vo_ref
):
    conv = pl.program_id(0)
    _, slots, span, width = k_ref.shape
    heads = width // HEAD
    _, tokens, query_width = out_ref.shape
    group = query_width // width
    done = tokens * group
    for h in range(heads):
        held = new_ref[h, 0:done].astype(F32)
        for g in range(group):
            at = (h * group + g) * HEAD
            out_ref[0, :, at : at + HEAD] = held[g * tokens : (g + 1) * tokens].astype(BF16)
    member = place[0] * COLUMNS + place[1]
    rotation = slots_ref[conv, 0] // slots
    slot, token = turn_slot(lengths[conv], rotation, member, slots, cycle, span)
    ko_ref[...] = k_ref[...]
    vo_ref[...] = v_ref[...]

    @pl.when((token > -span) & (token < turn))
    def _():
        row = lax.broadcasted_iota(I32, (span, HEAD), 0) + token
        inside = (row >= 0) & (row < turn)
        for h in range(heads):
            lanes = slice(h * HEAD, (h + 1) * HEAD)
            for i, (old, out) in enumerate(((k_ref, ko_ref), (v_ref, vo_ref))):
                start = done + i * span
                new = new_ref[h, start : start + span].astype(F32)
                kept = old[0, slot, :, lanes].astype(F32)
                out[0, slot, :, lanes] = jnp.where(inside, new, kept).astype(BF16)


def finish(place, lengths, span_slots, rows, cache_keys, cache_values, queries, turn, cycle):
    convs, slots, span, width = cache_keys.shape
    _, tokens, query_width = queries.shape
    spec = pl.BlockSpec((1, slots, span, width), lambda c: (c, 0, 0, 0))
    block = (rows.shape[0] // convs,) + rows.shape[1:]
    shape = jax.ShapeDtypeStruct(cache_keys.shape, BF16)
    return pl.pallas_call(
        functools.partial(finish_kernel, turn, cycle),
        grid=(convs,),
        in_specs=[SMEM] * 3 + [pl.BlockSpec(block, lambda c: (c, 0, 0)), spec, spec],
        out_specs=[pl.BlockSpec((1, tokens, query_width), lambda c: (c, 0, 0)), spec, spec],
        out_shape=[jax.ShapeDtypeStruct(queries.shape, BF16), shape, shape],
        compiler_params=pltpu.CompilerParams(vmem_limit_bytes=12 * MIB),
        cost_estimate=pl.CostEstimate(flops=0, bytes_accessed=5 * MIB, transcendentals=0),
        name="finish",
    )(place, lengths, span_slots, rows, cache_keys, cache_values)


def on_device(parts, queries, new_keys, new_values, cache_keys, cache_values, lengths, span_slots):
    _, slots, span, _ = cache_keys.shape
    cycle = parts * COLUMNS
    place = jnp.stack([lax.axis_index("z"), lax.axis_index("b")]).astype(I32)
    tie = lax.optimization_barrier

    turn_rows = pack_turn(queries, new_keys, new_values)
    turn_rows, cache_k, cache_v = tie((turn_rows, cache_keys, cache_values))
    turn_rows = lax.all_to_all(turn_rows, "b", 0, 0, tiled=True)
    first, second = pack_cache(cache_k, cache_v, (1, slots - 1))
    turn_rows, first, second = tie((turn_rows, first, second))
    first = lax.all_to_all(first, "b", 0, 0, tiled=True)

    message, new = ring_message(turn_rows)
    chunks = [None] * parts
    chunks[0] = message
    half = message.shape[0] // 2
    far = None

    def run(kv, distances, inits=None, after=(), joined=True):
        held = [c if isinstance(c, tuple) else (c,) for c in (chunks[d] for d in distances)]
        if after:
            held, _ = tie((held, after))
        inits = inits or [()] * len(distances)
        return attend(place, kv, held, distances, inits, parts, kv is far, joined)

    chunks[7], chunks[1] = shift(message, 1), shift(message, -1)
    second, chunks[7], chunks[1] = tie((second, chunks[7], chunks[1]))
    second = lax.all_to_all(second, "b", 0, 0, tiled=True)
    chunks[6], chunks[2] = shift(chunks[7], 1), shift(chunks[1], -1)
    near = prepare(place, lengths, span_slots, 0, first, cycle)
    n017 = run(near, (0, 1, 7))
    chunks[6], chunks[2], n017 = tie((chunks[6], chunks[2], n017))
    chunks[5], chunks[3] = shift(chunks[6], 1), shift(chunks[2], -1)
    chunks[4] = (shift(chunks[6][:half], 2), shift(chunks[2][half:], -2))
    n26 = run(near, (2, 6), after=(n017,))
    n435 = run(near, (4, 3, 5), after=(n26,))
    n435, second = tie((n435, second))
    far = prepare(place, lengths, span_slots, 1, second, cycle, new, near[0])

    (up4,) = run(far, (4,), (((n435, 0),),), joined=False)
    up3, down3 = run(far, (3, 5), (((n435, 1),), ((n435, 2),)), (up4,), False)
    up4, up3 = shift(up4, 2), shift(up3, 2)
    up2, down2 = run(far, (2, 6), (((n26, 0), (up4,)), ((n26, 1),)), (down3,), False)
    down3 = shift(down3, -2)
    up1, down1 = run(
        far, (1, 7), (((n017, 1), (up3,)), ((n017, 2), (down3,))), (up2,), False
    )
    up2, down2 = shift(up2, 2), shift(down2, -2)
    seen = [c if isinstance(c, tuple) else (c,) for c in chunks]
    seen, up2, down2 = tie((seen, up2, down2))
    rows = windows(place, lengths, span_slots, seen, slots, span, cycle)
    up1, down1 = shift(up1, 1), shift(down1, -1)
    (own,) = run(far, (0,), (((n017, 0),),), (rows,), False)
    rows = merge([own, up2, down2, up1, down1], rows)
    rows = lax.all_to_all(rows, "b", 0, 0, tiled=True)
    return finish(
        place,
        lengths,
        span_slots,
        rows,
        cache_keys,
        cache_values,
        queries,
        parts * HEAD // 2,
        cycle,
    )


def solution(mesh):
    members, heads, convs = mesh.devices.shape
    parts = members // COLUMNS
    grid = Mesh(mesh.devices.reshape(parts, COLUMNS, heads, convs), ("z", "b", "head", "conv"))
    ctx = ("z", "b")
    turn = P("conv", ctx, "head")
    cache = P("conv", ctx, None, "head")
    return jax.shard_map(
        functools.partial(on_device, parts),
        mesh=grid,
        in_specs=(turn, turn, turn, cache, cache, P("conv"), P("conv", None)),
        out_specs=(turn, cache, cache),
        check_vma=False,
    )
```

```python
import functools
import math

import jax
import jax.numpy as jnp
from jax import lax
from jax.experimental import pallas as pl
from jax.experimental.pallas import tpu as pltpu
from jax.sharding import Mesh, PartitionSpec as P

HEAD = 128
LOWEST = -1e30
SCALE = math.log2(math.e) / math.sqrt(HEAD)
F32, BF16, I32 = jnp.float32, jnp.bfloat16, jnp.int32
MIB = 2**20
EXTRA = 16
TILE = 512
COLUMNS = 8
SMEM = pl.BlockSpec(memory_space=pltpu.SMEM)
VMEM = pl.BlockSpec(memory_space=pltpu.VMEM)
ANY = pl.BlockSpec(memory_space=pl.ANY)
HBM = pl.BlockSpec(memory_space=pltpu.HBM)

def dot(a, b):
    return jnp.dot(a, b, preferred_element_type=F32)


def shift(a, by, size=8):
    return lax.ppermute(a, "z", [(i, (i + by) % size) for i in range(size)])


def pack_turn_kernel(*refs):
    sources, out_ref, held, sems = refs[:3], refs[3], refs[4:7], refs[7]
    copies = [
        pltpu.make_async_copy(source, target, sems.at[i])
        for i, (source, target) in enumerate(zip(sources, held))
    ]
    for copy in copies:
        copy.start()
    for copy in copies:
        copy.wait()
    q_ref, k_ref, v_ref = held
    convs, tokens, width = q_ref.shape
    heads = k_ref.shape[2] // HEAD
    group = width // (heads * HEAD)
    for c in range(convs):
        for h in range(heads):
            pieces = []
            for g in range(group):
                at = (h * group + g) * HEAD
                pieces.append(q_ref[c, :, at : at + HEAD])
            pieces.append(k_ref[c, :, h * HEAD : (h + 1) * HEAD])
            pieces.append(v_ref[c, :, h * HEAD : (h + 1) * HEAD])
            pieces = [piece.astype(F32) for piece in pieces]
            out_ref[c * heads + h] = jnp.concatenate(pieces, axis=0).astype(BF16)


def pack_turn(queries, new_keys, new_values):
    convs, tokens, width = queries.shape
    heads = new_keys.shape[2] // HEAD
    rows = tokens * (width // (heads * HEAD) + 2)
    return pl.pallas_call(
        pack_turn_kernel,
        in_specs=[HBM] * 3,
        out_specs=VMEM,
        out_shape=jax.ShapeDtypeStruct((convs * heads, rows, HEAD), BF16),
        scratch_shapes=[pltpu.VMEM(x.shape, BF16) for x in (queries, new_keys, new_values)]
        + [pltpu.SemaphoreType.DMA((3,))],
        compiler_params=pltpu.CompilerParams(vmem_limit_bytes=60 * MIB),
        name="pack_turn",
    )(queries, new_keys, new_values)


def ring_message_kernel(rows_ref, out_ref, new_ref):
    columns, count, _ = rows_ref.shape
    tokens = 8
    q_rows = count - 2 * tokens
    q = jnp.concatenate([rows_ref[s, 0:q_rows] for s in range(columns)], axis=0)
    news = [rows_ref[s, q_rows:].astype(F32) for s in range(columns)]
    new = [held[:tokens] for held in news] + [held[tokens:] for held in news]
    new = jnp.concatenate(new, axis=0).astype(BF16)
    out_ref[:, 0 : columns * q_rows] = q.T
    out_ref[:, columns * q_rows :] = new
    new_ref[...] = new


def ring_message(rows):
    columns, count, _ = rows.shape
    width = columns * (count - 16)
    return pl.pallas_call(
        ring_message_kernel,
        in_specs=[VMEM],
        out_specs=[VMEM, VMEM],
        out_shape=[
            jax.ShapeDtypeStruct((HEAD, width + HEAD), BF16),
            jax.ShapeDtypeStruct((HEAD, HEAD), BF16),
        ],
        compiler_params=pltpu.CompilerParams(vmem_limit_bytes=6 * MIB),
        name="ring_message",
    )(rows)


def pack_cache_kernel(keys_ref, values_ref, *rest):
    outs, sems = rest[:-1], rest[-1]
    convs, _, _, width = keys_ref.shape
    heads = width // HEAD
    copies = []
    for c in range(convs):
        for h in range(heads):
            for i, ref in enumerate((keys_ref, values_ref)):
                at = 0
                for out in outs:
                    copy = pltpu.make_async_copy(
                        ref.at[c, pl.ds(at, out.shape[2]), :, pl.ds(h * HEAD, HEAD)],
                        out.at[c * heads + h, i],
                        sems.at[len(copies)],
                    )
                    copy.start()
                    copies.append(copy)
                    at += out.shape[2]
    for copy in copies:
        copy.wait()


def pack_cache(cache_keys, cache_values, counts):
    convs, _, span, width = cache_keys.shape
    pairs = convs * width // HEAD
    return pl.pallas_call(
        pack_cache_kernel,
        in_specs=[HBM, HBM],
        out_specs=[VMEM] * len(counts),
        out_shape=[jax.ShapeDtypeStruct((pairs, 2, count, span, HEAD), BF16) for count in counts],
        scratch_shapes=[pltpu.SemaphoreType.DMA((2 * pairs * len(counts),))],
        compiler_params=pltpu.CompilerParams(vmem_limit_bytes=60 * MIB),
        name="pack_cache",
    )(cache_keys, cache_values)


def prepare_kernel(first_slot, cycle, place, lengths, slots_ref, kv, *refs):
    rest, keys, sums = refs[:-2], refs[-2], refs[-1]
    sources, _, slots, span, _ = kv.shape
    all_slots = slots_ref.shape[1] // cycle
    z, b = place[0], place[1]
    conv = b // (COLUMNS // 2)
    length = lengths[conv]
    rotation = slots_ref[conv, 0] // all_slots
    cached = sources * slots * span

    def base(source, slot):
        member = z * COLUMNS + source
        return (slot * cycle + lax.rem(member - rotation + cycle, cycle)) * span

    if rest:
        new_ref, known = rest
        filler = known[0:16, :].astype(F32)[0:1]
    else:
        first = kv[0, 0, 0, 0:16, :].astype(F32)[0:1]
        second = kv[1, 0, 0, 0:16, :].astype(F32)[0:1]
        filler = jnp.where(base(0, 0) < length, first, second)
    for source in range(sources):
        for slot in range(slots):
            left = length - base(source, first_slot + slot)
            start = (source * slots + slot) * span
            at = slice(start, start + span)
            rows = lax.broadcasted_iota(I32, (span, HEAD), 0) < left
            cols = lax.broadcasted_iota(I32, (HEAD, span), 1) < left
            keys[at, :] = jnp.where(rows, kv[source, 0, slot].astype(F32), filler).astype(BF16)
            turned = kv[source, 1, slot].T.astype(F32)
            sums[0:HEAD, at] = jnp.where(cols, turned, 0.0).astype(BF16)
            sums[HEAD:, at] = jnp.where(cols[:EXTRA], 1.0, 0.0).astype(BF16)
    if rest:
        turn_part = new_ref.shape[0] // 2
        keys[cached:, :] = new_ref[0:turn_part, :]
        sums[0:HEAD, cached:] = new_ref[turn_part:, :].T
        sums[HEAD:, cached:] = jnp.ones((EXTRA, turn_part), BF16)


def prepare(place, lengths, span_slots, first_slot, kv, cycle, new=None, known=None):
    positions = kv.shape[0] * kv.shape[2] * kv.shape[3]
    rest = []
    if new is not None:
        positions += new.shape[0] // 2
        rest = [new, known]
    return pl.pallas_call(
        functools.partial(prepare_kernel, first_slot, cycle),
        in_specs=[SMEM] * 3 + [VMEM] * (1 + len(rest)),
        out_specs=[VMEM] * 2,
        out_shape=[
            jax.ShapeDtypeStruct((positions, HEAD), BF16),
            jax.ShapeDtypeStruct((HEAD + EXTRA, positions), BF16),
        ],
        compiler_params=pltpu.CompilerParams(vmem_limit_bytes=12 * MIB),
        name="prepare",
    )(place, lengths, span_slots, kv, *rest)


def level_of(part):
    coded = part[HEAD:].astype(F32)
    return coded[0:1] + coded[1:2] + coded[2:3]


def combine(parts):
    levels = [level_of(part) for part in parts]
    top = functools.reduce(jnp.maximum, levels)
    shares = [jnp.exp2(level - top) for level in levels]
    total = functools.reduce(jnp.add, shares)
    sums = functools.reduce(
        jnp.add, [part[:HEAD].astype(F32) * share for part, share in zip(parts, shares)]
    )
    return sums, total, top


def attend_kernel(parts, distances, cuts, inits, with_new, *refs):
    count = len(distances)
    place, refs = refs[0], refs[1:]
    q_refs = []
    for pieces in cuts:
        q_refs.append(refs[:pieces])
        refs = refs[pieces:]
    picks = [pick for init in inits for pick in init]
    init_refs, refs = refs[: len(picks)], refs[len(picks) :]
    init_refs = [ref if pick is None else ref.at[pick] for ref, pick in zip(init_refs, picks)]
    keys, sums, outs = refs[0], refs[1], refs[2:]
    if len(outs[0].shape) == 3:
        outs = [outs[0].at[c] for c in range(count)]
    width = outs[0].shape[1]
    columns = count * width
    turn_part = width // 8
    cached = keys.shape[0] - with_new * turn_part
    z = place[0]

    q = [jnp.concatenate([ref[:, 0:width] for ref in held], axis=0) for held in q_refs]
    q = jnp.concatenate(q, axis=1).astype(F32) * SCALE
    high = q.astype(BF16)
    low = (q - high.astype(F32)).astype(BF16)
    q = jnp.concatenate([high, low], axis=0)
    tops, totals, at_init = [], [], 0
    for given in inits:
        if given:
            held, weight, level = combine(init_refs[at_init : at_init + len(given)])
            at_init += len(given)
            tops.append(level)
            totals.append(
                jnp.concatenate([held, jnp.broadcast_to(weight, (EXTRA, width))], axis=0)
            )
        else:
            tops.append(jnp.full((1, width), LOWEST, F32))
            totals.append(jnp.zeros((HEAD + EXTRA, width), F32))
    top = jnp.concatenate(tops, axis=1)
    total = jnp.concatenate(totals, axis=1)
    tile = TILE * 2 if count == 1 else TILE
    tiles = [slice(j, j + tile) for j in range(0, cached, tile)]
    if with_new:
        tiles.append(slice(cached, cached + turn_part))

    def scores_of(at):
        twice = jnp.concatenate([keys[at, :]] * 2, axis=1)
        scores = dot(twice, q)
        if at.start < cached:
            return scores
        row = lax.broadcasted_iota(I32, (turn_part, width), 0)
        lane = lax.broadcasted_iota(I32, (turn_part, width), 1)
        token = (lane // 64) * 8 + lax.rem(lane, 8)
        ahead = jnp.concatenate(
            [row - token + (z - lax.rem(z + d, parts)) * turn_part for d in distances], axis=1
        )
        return jnp.where(ahead <= 0, scores, LOWEST)

    scores = scores_of(tiles[0])
    for n, at in enumerate(tiles):
        following = scores_of(tiles[n + 1]) if n + 1 < len(tiles) else None
        higher = jnp.max(scores, axis=0, keepdims=True)
        if n > 0 or init_refs:
            higher = jnp.maximum(top, higher)
        weights = jnp.exp2(scores - higher).astype(BF16)
        share = dot(sums[:, at], weights)
        total = total * jnp.exp2(top - higher) + share if n > 0 or init_refs else share
        top, scores = higher, following
    denominator = total[HEAD : HEAD + 1]
    out = (total[:HEAD] * (1.0 / denominator)).astype(BF16)
    level = top + jnp.log2(denominator)
    first = level.astype(BF16).astype(F32)
    second = (level - first).astype(BF16).astype(F32)
    third = level - first - second
    row = lax.broadcasted_iota(I32, (EXTRA, columns), 0)
    coded = jnp.where(row == 0, first, jnp.where(row == 1, second, third)).astype(BF16)
    for c in range(count):
        at = slice(c * width, (c + 1) * width)
        outs[c][0:HEAD] = out[:, at]
        outs[c][HEAD:] = coded[:, at]


def attend(place, kv, chunks, distances, inits, parts, with_new, joined):
    keys, sums = kv
    count = len(distances)
    width = chunks[0][0].shape[1] - HEAD
    pieces = [piece for chunk in chunks for piece in chunk]
    cuts = [len(chunk) for chunk in chunks]
    given = [part[0] for init in inits for part in init]
    shape = jax.ShapeDtypeStruct((count,) * joined + (HEAD + EXTRA, width), BF16)
    picks = [[part[1] if len(part) > 1 else None for part in init] for init in inits]
    return pl.pallas_call(
        functools.partial(attend_kernel, parts, distances, cuts, picks, with_new),
        in_specs=[SMEM] + [VMEM] * (len(pieces) + len(given) + 2),
        out_specs=VMEM if joined else [VMEM] * count,
        out_shape=shape if joined else [shape] * count,
        compiler_params=pltpu.CompilerParams(vmem_limit_bytes=16 * MIB),
        cost_estimate=pl.CostEstimate(
            flops=8 * HEAD * count * width * keys.shape[0],
            bytes_accessed=3 * MIB,
            transcendentals=count * width * keys.shape[0],
        ),
        name="attend",
    )(place, *pieces, *given, keys, sums)


def merge_kernel(*refs):
    parts, window_ref, out_ref = refs[:-2], refs[-2], refs[-1]
    sums, total, _ = combine(parts)
    turned = (sums * (1.0 / total)).astype(BF16).T
    columns, rows, _ = out_ref.shape
    rows -= window_ref.shape[1]
    for s in range(columns):
        out_ref[s, 0:rows] = turned[s * rows : (s + 1) * rows]
        out_ref[s, rows:] = window_ref[s]


def merge(parts, windows):
    width = parts[0].shape[1]
    rows = width // COLUMNS + windows.shape[1]
    return pl.pallas_call(
        merge_kernel,
        in_specs=[VMEM] * (len(parts) + 1),
        out_specs=VMEM,
        out_shape=jax.ShapeDtypeStruct((COLUMNS, rows, HEAD), BF16),
        compiler_params=pltpu.CompilerParams(vmem_limit_bytes=8 * MIB),
        name="merge",
    )(*parts, windows)


def turn_slot(length, rotation, member, slots, cycle, span):
    j = lax.rem(member - rotation + cycle, cycle)
    slot = jnp.clip((length // span - j + cycle - 1) // cycle, 0, slots - 1)
    return slot, (j + slot * cycle) * span - length


def windows_kernel(slots, span, cycle, place, lengths, slots_ref, *refs):
    news, out_ref, rows = refs[:-2], refs[-2], refs[-1]
    turn_part = HEAD // 2
    chunks, at = [], 0
    while at < len(news):
        if news[at].shape[0] > turn_part:
            chunks.append((news[at].at[0:turn_part], news[at].at[turn_part:]))
            at += 1
        else:
            chunks.append((news[at], news[at + 1]))
            at += 2
    parts = len(chunks)
    width = news[0].shape[1] - HEAD
    turn = parts * turn_part
    z, b = place[0], place[1]
    conv = b // (COLUMNS // 2)
    rotation = slots_ref[conv, 0] // slots
    edge = jnp.zeros((span, 2 * HEAD), F32)
    rows[0:span] = edge
    rows[span + turn : turn + 2 * span] = edge
    rows[turn + 2 * span :] = edge[0:8]
    for d, chunk in enumerate(chunks):
        start = pl.multiple_of(span + lax.rem(z + d, parts) * turn_part, turn_part)
        rows[pl.ds(start, turn_part), 0:HEAD] = chunk[0][:, width:].astype(F32)
        rows[pl.ds(start, turn_part), HEAD:] = chunk[1][:, width:].astype(F32)
    for to in range(COLUMNS):
        _, token = turn_slot(lengths[conv], rotation, z * COLUMNS + to, slots, cycle, span)
        start = jnp.clip(token + span, 0, turn + span)
        whole = pl.multiple_of(start // 8 * 8, 8)
        window = rows[pl.ds(whole, span + 8), :]
        window = pltpu.roll(window, lax.rem(span + 8 + whole - start, span + 8), 0)
        window = window[0:span].astype(BF16)
        out_ref[to, 0:span] = window[:, 0:HEAD]
        out_ref[to, span:] = window[:, HEAD:]


def windows(place, lengths, span_slots, chunks, slots, span, cycle):
    turn = len(chunks) * HEAD // 2
    pieces = [piece for chunk in chunks for piece in chunk]
    return pl.pallas_call(
        functools.partial(windows_kernel, slots, span, cycle),
        in_specs=[SMEM] * 3 + [VMEM] * len(pieces),
        out_specs=VMEM,
        out_shape=jax.ShapeDtypeStruct((COLUMNS, 2 * span, HEAD), BF16),
        scratch_shapes=[pltpu.VMEM((turn + 2 * span + 8, 2 * HEAD), F32)],
        compiler_params=pltpu.CompilerParams(vmem_limit_bytes=8 * MIB),
        name="windows",
    )(place, lengths, span_slots, *pieces)


def finish_kernel(
    turn, cycle, place, lengths, slots_ref, new_ref, k_ref, v_ref, out_ref, ko_ref, vo_ref
):
    conv = pl.program_id(0)
    _, slots, span, width = k_ref.shape
    heads = width // HEAD
    _, tokens, query_width = out_ref.shape
    group = query_width // width
    done = tokens * group
    for h in range(heads):
        held = new_ref[h, 0:done].astype(F32)
        for g in range(group):
            at = (h * group + g) * HEAD
            out_ref[0, :, at : at + HEAD] = held[g * tokens : (g + 1) * tokens].astype(BF16)
    member = place[0] * COLUMNS + place[1]
    rotation = slots_ref[conv, 0] // slots
    slot, token = turn_slot(lengths[conv], rotation, member, slots, cycle, span)
    ko_ref[...] = k_ref[...]
    vo_ref[...] = v_ref[...]

    @pl.when((token > -span) & (token < turn))
    def _():
        row = lax.broadcasted_iota(I32, (span, HEAD), 0) + token
        inside = (row >= 0) & (row < turn)
        for h in range(heads):
            lanes = slice(h * HEAD, (h + 1) * HEAD)
            for i, (old, out) in enumerate(((k_ref, ko_ref), (v_ref, vo_ref))):
                start = done + i * span
                new = new_ref[h, start : start + span].astype(F32)
                kept = old[0, slot, :, lanes].astype(F32)
                out[0, slot, :, lanes] = jnp.where(inside, new, kept).astype(BF16)


def finish(place, lengths, span_slots, rows, cache_keys, cache_values, queries, turn, cycle):
    convs, slots, span, width = cache_keys.shape
    _, tokens, query_width = queries.shape
    spec = pl.BlockSpec((1, slots, span, width), lambda c: (c, 0, 0, 0))
    block = (rows.shape[0] // convs,) + rows.shape[1:]
    shape = jax.ShapeDtypeStruct(cache_keys.shape, BF16)
    return pl.pallas_call(
        functools.partial(finish_kernel, turn, cycle),
        grid=(convs,),
        in_specs=[SMEM] * 3 + [pl.BlockSpec(block, lambda c: (c, 0, 0)), spec, spec],
        out_specs=[pl.BlockSpec((1, tokens, query_width), lambda c: (c, 0, 0)), spec, spec],
        out_shape=[jax.ShapeDtypeStruct(queries.shape, BF16), shape, shape],
        compiler_params=pltpu.CompilerParams(vmem_limit_bytes=12 * MIB),
        cost_estimate=pl.CostEstimate(flops=0, bytes_accessed=5 * MIB, transcendentals=0),
        name="finish",
    )(place, lengths, span_slots, rows, cache_keys, cache_values)


def on_device(parts, queries, new_keys, new_values, cache_keys, cache_values, lengths, span_slots):
    _, slots, span, _ = cache_keys.shape
    cycle = parts * COLUMNS
    place = jnp.stack([lax.axis_index("z"), lax.axis_index("b")]).astype(I32)
    tie = lax.optimization_barrier

    turn_rows = pack_turn(queries, new_keys, new_values)
    turn_rows, cache_k, cache_v = tie((turn_rows, cache_keys, cache_values))
    turn_rows = lax.all_to_all(turn_rows, "b", 0, 0, tiled=True)
    first, second = pack_cache(cache_k, cache_v, (1, slots - 1))
    turn_rows, first, second = tie((turn_rows, first, second))
    first = lax.all_to_all(first, "b", 0, 0, tiled=True)

    message, new = ring_message(turn_rows)
    chunks = [None] * parts
    chunks[0] = message
    half = message.shape[0] // 2
    far = None

    def run(kv, distances, inits=None, after=(), joined=True):
        held = [c if isinstance(c, tuple) else (c,) for c in (chunks[d] for d in distances)]
        if after:
            held, _ = tie((held, after))
        inits = inits or [()] * len(distances)
        return attend(place, kv, held, distances, inits, parts, kv is far, joined)

    chunks[7], chunks[1] = shift(message, 1), shift(message, -1)
    second, chunks[7], chunks[1] = tie((second, chunks[7], chunks[1]))
    second = lax.all_to_all(second, "b", 0, 0, tiled=True)
    chunks[6], chunks[2] = shift(chunks[7], 1), shift(chunks[1], -1)
    near = prepare(place, lengths, span_slots, 0, first, cycle)
    n017 = run(near, (0, 1, 7))
    chunks[6], chunks[2], n017 = tie((chunks[6], chunks[2], n017))
    chunks[5], chunks[3] = shift(chunks[6], 1), shift(chunks[2], -1)
    chunks[4] = (shift(chunks[6][:half], 2), shift(chunks[2][half:], -2))
    n26 = run(near, (2, 6), after=(n017,))
    n435 = run(near, (4, 3, 5), after=(n26,))
    n435, second = tie((n435, second))
    far = prepare(place, lengths, span_slots, 1, second, cycle, new, near[0])

    (up4,) = run(far, (4,), (((n435, 0),),), joined=False)
    up3, down3 = run(far, (3, 5), (((n435, 1),), ((n435, 2),)), (up4,), False)
    up4, up3 = shift(up4, 2), shift(up3, 2)
    up2, down2 = run(far, (2, 6), (((n26, 0), (up4,)), ((n26, 1),)), (down3,), False)
    down3 = shift(down3, -2)
    up1, down1 = run(
        far, (1, 7), (((n017, 1), (up3,)), ((n017, 2), (down3,))), (up2,), False
    )
    up2, down2 = shift(up2, 2), shift(down2, -2)
    seen = [c if isinstance(c, tuple) else (c,) for c in chunks]
    seen, up2, down2 = tie((seen, up2, down2))
    rows = windows(place, lengths, span_slots, seen, slots, span, cycle)
    up1, down1 = shift(up1, 1), shift(down1, -1)
    (own,) = run(far, (0,), (((n017, 0),),), (rows,), False)
    rows = merge([own, up2, down2, up1, down1], rows)
    rows = lax.all_to_all(rows, "b", 0, 0, tiled=True)
    return finish(
        place,
        lengths,
        span_slots,
        rows,
        cache_keys,
        cache_values,
        queries,
        parts * HEAD // 2,
        cycle,
    )


def solution(mesh):
    members, heads, convs = mesh.devices.shape
    parts = members // COLUMNS
    grid = Mesh(mesh.devices.reshape(parts, COLUMNS, heads, convs), ("z", "b", "head", "conv"))
    ctx = ("z", "b")
    turn = P("conv", ctx, "head")
    cache = P("conv", ctx, None, "head")
    return jax.shard_map(
        functools.partial(on_device, parts),
        mesh=grid,
        in_specs=(turn, turn, turn, cache, cache, P("conv"), P("conv", None)),
        out_specs=(turn, cache, cache),
        check_vma=False,
    )
```
